256 devices in a mesh: seq: 32 (over y, x, core), tp: 8 (over z).
Axes of the slice: x: 4, y: 4, z: 8, core: 2. Of those that a mesh axis runs over, the one named last changes fastest.
Arguments:
- token_ids: int32 [2, 2, 8], replicated, may hold values from 0 to 65535
- lengths: int32 [2], replicated, may hold values from 1 to 131072, as said below
- norm_gain: bfloat16 [8192], P('seq'), may hold values from 0.099609375 to 1.8984375
- emb_table: bfloat16 [65536, 8192], P(('seq', 'tp')), may hold values from -6 to 6
- q_weight: bfloat16 [8192, 8192], P('seq', 'tp'), may hold values from -0.0625 to 0.0625
- key_matrix: bfloat16 [8192, 1024], P('seq', 'tp'), may hold values from -0.26367188 to 0.26367188
- value_matrix: bfloat16 [8192, 1024], P('seq', 'tp'), may hold values from -0.0625 to 0.0625
- o_weight: bfloat16 [8192, 8192], P('tp', 'seq'), may hold values from -0.0625 to 0.0625
- key_cache: bfloat16 [2, 131072, 8, 128], P(None, 'seq', 'tp'), may hold values from -160 to 160
- value_cache: bfloat16 [2, 131072, 8, 128], P(None, 'seq', 'tp'), may hold values from -12 to 12
Outputs:
- attention_out: bfloat16 [32, 8192], P('tp', 'seq')
The draws below stay inside these ranges and needn't reach their ends.
Inputs may be any that keep to these rules, and one draw needn't show every extreme that they name: `lengths`: every game's history has at least one position; at least one game's history fills all 131072 cache positions.
All inputs are finite; a program needn't handle non-finite values.
Results may differ from the reference program's by a relative error of at most 0.019.
The reference program's roundings to bfloat16 on the way count: a program that leaves them out, or rounds other values in their place, can miss the bound.
Values may be sent and summed in bfloat16 or wider, within the bound.
A program may use at most 64 MiB of HBM per device.

```python
import jax
import jax.numpy as jnp
import numpy as np
from jax import lax

MODEL_WIDTH = 8192
QUERY_HEADS = 64
KEY_HEADS = 8
HEAD_SIZE = 128
VOCAB = 65536
GAME_COUNT = 2
CANDIDATE_MOVES = 8
NEW_TOKENS = 2
CACHE_SLOTS = 131072


def draw_lengths(key, part):
    key = jax.random.fold_in(key, 13)
    pick_key, other_key = jax.random.split(key)
    full_game = jax.random.randint(pick_key, (), 0, GAME_COUNT)
    others = jax.random.randint(other_key, (GAME_COUNT,), 1, CACHE_SLOTS + 1)
    return jnp.where(jnp.arange(GAME_COUNT, dtype=jnp.int32) == full_game, CACHE_SLOTS, others).astype(jnp.int32)


def draw_key_cache(key, part):
    key = jax.random.fold_in(key, 11)
    noise_seed_key, scale_seed_key = jax.random.split(key)
    random_noise = jnp.clip(jax.random.normal(noise_seed_key, (GAME_COUNT, CACHE_SLOTS // 8, 8, KEY_HEADS, HEAD_SIZE), jnp.float32), -4.0, 4.0)
    upper_limit = 2.0
    block_scaling = jnp.exp(jax.random.uniform(scale_seed_key, (GAME_COUNT, CACHE_SLOTS // 8, 1, KEY_HEADS, 1), jnp.float32, jnp.log(0.2), jnp.log(upper_limit)))
    return (random_noise * block_scaling).reshape(GAME_COUNT, CACHE_SLOTS, KEY_HEADS, HEAD_SIZE).astype(jnp.bfloat16)


def draw_value_cache(key, part):
    key = jax.random.fold_in(key, 12)
    noise_seed_key, scale_seed_key = jax.random.split(key)
    random_noise = jnp.clip(jax.random.normal(noise_seed_key, (GAME_COUNT, CACHE_SLOTS // 8, 8, KEY_HEADS, HEAD_SIZE), jnp.float32), -4.0, 4.0)
    upper_limit = 3.0
    block_scaling = jnp.exp(jax.random.uniform(scale_seed_key, (GAME_COUNT, CACHE_SLOTS // 8, 1, KEY_HEADS, 1), jnp.float32, jnp.log(0.3), jnp.log(upper_limit)))
    return (random_noise * block_scaling).reshape(GAME_COUNT, CACHE_SLOTS, KEY_HEADS, HEAD_SIZE).astype(jnp.bfloat16)


def with_ends(entries, rng, least, largest):
    shape = entries.shape
    place = [jax.random.randint(jax.random.fold_in(rng, axis), (), 0, shape[axis]) for axis in range(len(shape))]
    entries = entries.at[tuple(place)].set(least)
    longest = shape.index(max(shape))
    place[longest] = (place[longest] + 1) % shape[longest]
    return entries.at[tuple(place)].set(largest)


def shard_levels(key, shape, cuts, low, largest):
    loudness, own = 1.0, jax.random.fold_in(key, 6)
    for dim, blocks in cuts:
        heights = jnp.exp(jax.random.uniform(jax.random.fold_in(own, dim), (blocks,), jnp.float32, low / len(cuts), largest / len(cuts)))
        loudness = loudness * jnp.repeat(heights, shape[dim] // blocks).reshape([-1 if axis == dim else 1 for axis in range(len(shape))])
    return loudness


def bell_draw(rng, shape, scale, limit, cuts=(), kind=jnp.bfloat16):
    values = scale * jax.random.normal(rng, shape, jnp.float32)
    if cuts:
        values = values * shard_levels(rng, shape, cuts, -0.22, 0.18)
    return jnp.clip(values, -limit, limit).astype(kind)


def setup_inputs(seed: int = 0) -> dict:
    key_of = jax.random.split(jax.random.key(seed), 11)
    token_ids = with_ends(jax.random.randint(key_of[0], (NEW_TOKENS, GAME_COUNT, CANDIDATE_MOVES), 0, VOCAB), jax.random.fold_in(key_of[0], 1), 0, VOCAB - 1).astype(jnp.int32)
    lengths = draw_lengths(jax.random.fold_in(key_of[10], 71), 0)
    norm_gain = jnp.clip(1.0 + 0.18 * jax.random.normal(key_of[2], (MODEL_WIDTH,), jnp.float32), 0.099609375, 1.8984375).astype(jnp.bfloat16)
    emb_table = bell_draw(key_of[3], (VOCAB, MODEL_WIDTH), 1.0, 6.0, ((0, 256),))
    q_weight = bell_draw(key_of[4], (MODEL_WIDTH, QUERY_HEADS * HEAD_SIZE), MODEL_WIDTH ** -0.5, 0.0625, ((0, 32), (1, 8)))
    key_matrix = bell_draw(key_of[5], (MODEL_WIDTH, KEY_HEADS * HEAD_SIZE), (4.0 * MODEL_WIDTH ** -0.5), 0.26367188, ((0, 32), (1, 8)))
    value_matrix = bell_draw(key_of[6], (MODEL_WIDTH, KEY_HEADS * HEAD_SIZE), MODEL_WIDTH ** -0.5, 0.0625, ((0, 32), (1, 8)))
    o_weight = bell_draw(key_of[7], (QUERY_HEADS * HEAD_SIZE, MODEL_WIDTH), (QUERY_HEADS * HEAD_SIZE) ** -0.5, 0.0625, ((0, 8), (1, 32)))
    key_cache = draw_key_cache(jax.random.fold_in(key_of[10], 71), 0)
    value_cache = draw_value_cache(jax.random.fold_in(key_of[10], 71), 0)
    return {"token_ids": token_ids, "lengths": lengths, "norm_gain": norm_gain, "emb_table": emb_table, "q_weight": q_weight, "key_matrix": key_matrix, "value_matrix": value_matrix, "o_weight": o_weight, "key_cache": key_cache, "value_cache": value_cache}


EPSILON = 1e-05
FLOOR = -1e+30

def rotary_rates(head_dim):
    half_dim = head_dim // 2
    plain_rate = 500000.0 ** (-(np.arange(half_dim) * 2.0) / head_dim)
    wave_len = 2.0 * np.pi / plain_rate
    blend = (8192.0 / wave_len - 1.0) / 3.0
    scaled = np.where(wave_len < 2048.0, plain_rate, np.where(wave_len > 8192.0, plain_rate / 8.0, (1.0 - blend) * plain_rate / 8.0 + blend * plain_rate))
    return jnp.asarray(scaled, dtype=jnp.float32)

def rotate(vectors, angles):
    half_dim = vectors.shape[-1] // 2
    cosine = jnp.cos(angles)
    sine = jnp.sin(angles)
    first = vectors[..., :half_dim]
    second = vectors[..., half_dim:]
    return jnp.concatenate([first * cosine - second * sine, second * cosine + first * sine], axis=-1)

def finish(query_sum, key_sum, value_sum, square_sum, positions):
    inv_rms = lax.rsqrt(square_sum / MODEL_WIDTH + EPSILON)[:, None]
    angles = positions.astype(jnp.float32)[:, None, None] * rotary_rates(HEAD_SIZE)[None, None, :]
    counted = query_sum.shape[0]
    query_rows = rotate((query_sum * inv_rms).reshape(counted, -1, HEAD_SIZE), angles).astype(jnp.bfloat16).reshape(counted, -1)
    recent_keys = rotate((key_sum * inv_rms).reshape(counted, -1, HEAD_SIZE), angles).astype(jnp.bfloat16).reshape(counted, -1)
    recent_values = (value_sum * inv_rms).astype(jnp.bfloat16)
    return (query_rows, recent_keys, recent_values)

def combine_parts(earlier, later):
    highest = jnp.maximum(earlier[0], later[0])
    first_scale = jnp.exp(earlier[0] - highest)
    second_scale = jnp.exp(later[0] - highest)
    return (highest, first_scale * earlier[1] + second_scale * later[1], first_scale[..., None] * earlier[2] + second_scale[..., None] * later[2])

def fresh_portion(query_groups, recent_keys, recent_values, head_count):
    scale = HEAD_SIZE ** (-0.5)
    fresh_keys = recent_keys.reshape(NEW_TOKENS, GAME_COUNT, CANDIDATE_MOVES, head_count, HEAD_SIZE).astype(jnp.float32)
    fresh_values = recent_values.reshape(NEW_TOKENS, GAME_COUNT, CANDIDATE_MOVES, head_count, HEAD_SIZE).astype(jnp.float32)
    scores = jnp.einsum('agchjd,bgchd->agchjb', query_groups.astype(jnp.float32), fresh_keys) * scale
    causal = (jnp.arange(NEW_TOKENS, dtype=jnp.int32)[:, None] >= jnp.arange(NEW_TOKENS, dtype=jnp.int32)[None, :])[:, None, None, None, None, :]
    masked = jnp.where(causal, scores, FLOOR)
    highest = lax.optimization_barrier(jnp.max(masked, axis=-1))
    shifted = jnp.where(causal, jnp.exp(masked - highest[..., None]), 0.0)
    totals = lax.optimization_barrier(jnp.sum(shifted, axis=-1))
    summed = jnp.einsum('agchjb,bgchd->agchjd', shifted.astype(jnp.bfloat16).astype(jnp.float32), fresh_values)
    highest = highest.transpose(1, 3, 0, 2, 4).reshape(GAME_COUNT, head_count, -1)
    totals = totals.transpose(1, 3, 0, 2, 4).reshape(GAME_COUNT, head_count, -1)
    summed = summed.transpose(1, 3, 0, 2, 4, 5).reshape(GAME_COUNT, head_count, -1, HEAD_SIZE)
    return (highest, totals, summed)

def reference(token_ids, lengths, norm_gain, emb_table, q_weight, key_matrix, value_matrix, o_weight, key_cache, value_cache):
    count_of_rows = NEW_TOKENS * GAME_COUNT * CANDIDATE_MOVES
    group_size = QUERY_HEADS // KEY_HEADS
    scale = HEAD_SIZE ** (-0.5)
    embedded = jnp.take(emb_table, token_ids.reshape(count_of_rows).astype(jnp.int32), axis=0).astype(jnp.float32)
    square_sum = lax.optimization_barrier(jnp.sum(embedded * embedded, axis=-1))
    normed = (embedded * norm_gain.astype(jnp.float32)).astype(jnp.bfloat16)
    query_sum = jnp.dot(normed, q_weight, preferred_element_type=jnp.float32)
    key_sum = jnp.dot(normed, key_matrix, preferred_element_type=jnp.float32)
    value_sum = jnp.dot(normed, value_matrix, preferred_element_type=jnp.float32)
    positions = (lengths[None, :, None] + jnp.arange(NEW_TOKENS, dtype=jnp.int32)[:, None, None] + jnp.zeros((NEW_TOKENS, GAME_COUNT, CANDIDATE_MOVES), jnp.int32)).reshape(count_of_rows)
    query_rows, recent_keys, recent_values = finish(query_sum, key_sum, value_sum, square_sum, positions)
    query_groups = query_rows.reshape(NEW_TOKENS, GAME_COUNT, CANDIDATE_MOVES, KEY_HEADS, group_size, HEAD_SIZE)
    per_head_split = query_groups.transpose(3, 1, 0, 2, 4, 5).reshape(KEY_HEADS, GAME_COUNT, -1, HEAD_SIZE)
    live = (jnp.arange(CACHE_SLOTS, dtype=jnp.int32)[None, :] < lengths[:, None])[:, None, :]

    def single_head(head):
        grouped = lax.dynamic_index_in_dim(per_head_split, head, 0, keepdims=False).astype(jnp.float32)
        keys = lax.dynamic_index_in_dim(key_cache, head, 2, keepdims=False).astype(jnp.float32)
        values = lax.dynamic_index_in_dim(value_cache, head, 2, keepdims=False).astype(jnp.float32)
        scores = jnp.einsum('gqd,gkd->gqk', grouped, keys) * scale
        masked = jnp.where(live, scores, FLOOR)
        highest = lax.optimization_barrier(jnp.max(masked, axis=-1))
        shifted = jnp.where(live, jnp.exp(masked - highest[..., None]), 0.0)
        summed = jnp.einsum('gqk,gkd->gqd', shifted.astype(jnp.bfloat16).astype(jnp.float32), values)
        return (highest, lax.optimization_barrier(jnp.sum(shifted, axis=-1)), summed)
    cache_peak, cache_denominator, cache_result = lax.map(single_head, jnp.arange(KEY_HEADS, dtype=jnp.int32))
    cache_portion = (cache_peak.transpose(1, 0, 2), cache_denominator.transpose(1, 0, 2), cache_result.transpose(1, 0, 2, 3))
    merged_output = combine_parts(cache_portion, fresh_portion(query_groups, recent_keys, recent_values, KEY_HEADS))
    context_vectors = (merged_output[2] / merged_output[1][..., None]).astype(jnp.bfloat16)
    context_vectors = context_vectors.reshape(GAME_COUNT, KEY_HEADS, NEW_TOKENS, CANDIDATE_MOVES, group_size, HEAD_SIZE).transpose(2, 0, 3, 1, 4, 5).reshape(count_of_rows, QUERY_HEADS * HEAD_SIZE)
    return jnp.dot(context_vectors, o_weight, preferred_element_type=jnp.float32).astype(jnp.bfloat16)
```

```python
import functools

import jax
import jax.numpy as jnp
import numpy as np
from jax import lax
from jax.experimental import pallas as pl
from jax.experimental.pallas import tpu as pltpu
from jax.sharding import PartitionSpec as P

MODEL_WIDTH = 8192
QUERY_HEADS = 64
KEY_HEADS = 8
HEAD_SIZE = 128
GAME_COUNT = 2
CANDIDATE_MOVES = 8
NEW_TOKENS = 2
ROWS = NEW_TOKENS * GAME_COUNT * CANDIDATE_MOVES
GROUP = QUERY_HEADS // KEY_HEADS

EPSILON = 1e-05
FLOOR = -1e30
LOWEST = -1e29
LOG2E = 1.4426950408889634
MESH = pl.DeviceIdType.MESH
F32 = jnp.float32
BF16 = jnp.bfloat16


def rotary_rates(head_dim):
    half_dim = head_dim // 2
    plain_rate = 500000.0 ** (-(np.arange(half_dim) * 2.0) / head_dim)
    wave_len = 2.0 * np.pi / plain_rate
    blend = (8192.0 / wave_len - 1.0) / 3.0
    scaled = np.where(
        wave_len < 2048.0,
        plain_rate,
        np.where(
            wave_len > 8192.0,
            plain_rate / 8.0,
            (1.0 - blend) * plain_rate / 8.0 + blend * plain_rate,
        ),
    )
    return np.concatenate([scaled, scaled]).astype(np.float32).reshape(1, head_dim)


def rounded(x):
    return x.astype(BF16).astype(F32)


def in_three(x):
    high = rounded(x)
    middle = rounded(x - high)
    return high, middle, rounded(x - high - middle)


def kernel(
    ids,
    lengths,
    gain,
    rates,
    emb,
    q_weight,
    key_matrix,
    value_matrix,
    o_weight,
    key_cache,
    value_cache,
    out,
    table,
    qw,
    kw,
    vw,
    ow,
    kc,
    vc,
    send1,
    recv1,
    send2,
    recv2,
    spread,
    send3,
    recv3,
    rows,
    send5,
    recv5,
    send6,
    recv6,
    send7,
    recv7,
    table_sems,
    load_sems,
    send_sems,
    recv_sems,
):
    seq, tp = lax.axis_size("seq"), lax.axis_size("tp")
    s, t = lax.axis_index("seq"), lax.axis_index("tp")
    width = gain.shape[0]
    vocab_local = emb.shape[0]
    shard_len = key_cache.shape[1]
    scale = HEAD_SIZE ** (-0.5)

    y, x, core = lax.div(s, 8), lax.rem(lax.div(s, 2), 4), lax.rem(s, 2)

    def moved(dy, dx, dc):
        return (lax.rem(y + dy, 4) * 4 + lax.rem(x + dx, 4)) * 2 + lax.rem(core + dc, 2)

    steps = [(dy, dx, dc) for dy in range(4) for dx in range(4) for dc in range(2)]
    steps.sort(key=lambda d: -10 * (min(d[0], 4 - d[0]) + min(d[1], 4 - d[1])) - d[2])
    seq_peers = [moved(*d) for d in steps[:-1]]
    tp_peers = [lax.rem(t + d, tp) for d in (4, 3, 5, 2, 6, 1, 7)]

    barrier = pltpu.get_barrier_semaphore()

    for device in [(peer, t) for peer in seq_peers] + [(s, peer) for peer in tp_peers]:
        pl.semaphore_signal(barrier, inc=1, device_id=device, device_id_type=MESH)

    def table_copy(chunk):
        return pltpu.make_async_copy(
            emb.at[:, pl.ds(pl.multiple_of(chunk * width, width), width)],
            table.at[chunk],
            table_sems.at[chunk],
        )

    for peer in seq_peers + [s]:
        table_copy(peer).start()
    loads = [
        pltpu.make_async_copy(src, dst, load_sems.at[i])
        for i, (src, dst) in enumerate(
            [
                (q_weight, qw),
                (key_matrix, kw),
                (value_matrix, vw),
                (key_cache, kc),
                (value_cache, vc),
                (o_weight, ow),
            ]
        )
    ]
    pending, loaded = [], set()

    def need(*names):
        for i in names:
            loads[i].wait()
            loaded.add(i)

    first_id = (s * tp + t) * vocab_local
    row_of = lax.broadcasted_iota(jnp.int32, (ROWS, vocab_local), 0)
    wanted = jnp.full((ROWS, vocab_local), -1, jnp.int32)
    for r in range(ROWS):
        token = ids[r // 16, (r // 8) % 2, r % 8]
        wanted = jnp.where(row_of == r, token - first_id, wanted)
    one_hot = jnp.where(
        wanted == lax.broadcasted_iota(jnp.int32, (ROWS, vocab_local), 1), 1.0, 0.0
    ).astype(BF16)

    def picked(chunk):
        table_copy(chunk).wait()
        return jnp.dot(one_hot, table[chunk], preferred_element_type=F32).astype(BF16)

    def scatter_copy(phase, source, target, device):
        return pltpu.make_async_remote_copy(
            src_ref=source,
            dst_ref=target,
            send_sem=send_sems.at[phase],
            recv_sem=recv_sems.at[phase],
            device_id=device,
            device_id_type=MESH,
        )

    def await_all(phase, buffer, count):
        part = buffer.at[pl.ds(0, count)]
        pltpu.make_async_copy(part, part, recv_sems.at[phase]).wait()

    def await_sent(phase, buffer, count):
        part = buffer.at[pl.ds(0, count)]
        pltpu.make_async_copy(part, part, send_sems.at[phase]).wait()

    pl.semaphore_wait(barrier, seq + tp - 2)

    for peer in seq_peers:
        send1[peer] = picked(peer)
        scatter_copy(0, send1.at[peer], recv1.at[s], (peer, t)).start()
    pending.append(lambda: await_sent(0, send1, seq - 1))
    recv1[s] = picked(s)
    for load in loads:
        load.start()
    await_all(0, recv1, seq - 1)

    found = jnp.sum(recv1[...].astype(F32), axis=0).astype(BF16)
    send2[...] = found

    for peer in tp_peers:
        scatter_copy(1, send2, recv2.at[t], (s, peer)).start()
    pending.append(lambda: await_sent(1, recv2, tp - 1))
    recv2[t] = found
    await_all(1, recv2, tp - 1)
    embedded = jnp.sum(recv2[...].astype(F32), axis=0)

    squares = jnp.sum(embedded * embedded, axis=-1, keepdims=True)
    normed = (embedded * gain[...].astype(F32)[None, :]).astype(BF16)
    need(0, 1, 2)
    query_part = jnp.dot(normed, qw[...], preferred_element_type=F32)
    key_part = jnp.dot(normed, kw[...], preferred_element_type=F32)
    value_part = jnp.dot(normed, vw[...], preferred_element_type=F32)
    for j in range(GROUP):
        spread[pl.ds(j, ROWS, stride=16), :] = query_part[:, j * HEAD_SIZE : (j + 1) * HEAD_SIZE]
    spread[pl.ds(8, ROWS, stride=16), :] = key_part
    spread[pl.ds(9, ROWS, stride=16), :] = value_part
    for j in range(10, 16):
        spread[pl.ds(j, ROWS, stride=16), :] = jnp.broadcast_to(squares, (ROWS, HEAD_SIZE))
    send3[...] = spread[...].reshape(ROWS, 16, HEAD_SIZE).astype(BF16)

    for peer in seq_peers:
        scatter_copy(2, send3.at[peer], recv3.at[s], (peer, t)).start()
    pending.append(lambda: await_sent(2, send3, seq - 1))
    recv3[s] = send3[s]
    game = lax.rem(lax.div(s, CANDIDATE_MOVES), GAME_COUNT)
    step = lax.div(s, GAME_COUNT * CANDIDATE_MOVES)
    position = (lengths[game] + step).astype(F32)
    angles = position * rates[...]
    lane = lax.broadcasted_iota(jnp.int32, (1, HEAD_SIZE), 1)
    cosine = jnp.cos(angles)
    sine = jnp.sin(angles)
    sine = jnp.where(lane < HEAD_SIZE // 2, -sine, sine)
    await_all(2, recv3, seq - 1)

    sums = jnp.sum(recv3[...].astype(F32), axis=0)
    inv_rms = lax.rsqrt(sums[10:11, :] / MODEL_WIDTH + EPSILON)
    scaled = sums * inv_rms
    turned = scaled * cosine + pltpu.roll(scaled, HEAD_SIZE // 2, 1) * sine
    place = lax.broadcasted_iota(jnp.int32, (16, HEAD_SIZE), 0)
    own = jnp.where(place < 9, turned, scaled).astype(BF16)
    rows[s] = own

    for peer in seq_peers:
        scatter_copy(3, rows.at[s], rows.at[s], (peer, t)).start()
    pending.append(lambda: await_sent(3, rows, seq - 1))
    own_queries = own.astype(F32)[:8, :]
    need(3, 4)
    await_all(3, rows, seq - 1)

    factor = scale * LOG2E
    for g in range(GAME_COUNT):
        halves = [
            rows[pl.ds(16 * a + 8 * g, 8)].astype(F32)[:, :8, :].reshape(64, HEAD_SIZE)
            for a in range(NEW_TOKENS)
        ]
        queries = jnp.concatenate(halves, axis=0).astype(BF16)
        scores = lax.dot_general(
            queries, kc[g], (((1,), (1,)), ((), ())), preferred_element_type=F32
        )
        slot = s * shard_len + lax.broadcasted_iota(jnp.int32, (1, shard_len), 1)
        masked = jnp.where(slot < lengths[g], scores * factor, FLOOR)
        top = jnp.maximum(jnp.max(masked, axis=-1, keepdims=True), LOWEST)
        shifted = jnp.exp2(masked - top)
        total = jnp.sum(shifted, axis=-1, keepdims=True)
        summed = jnp.dot(shifted.astype(BF16), vc[g], preferred_element_type=F32)
        lanes = lax.broadcasted_iota(jnp.int32, (128, HEAD_SIZE), 1)
        packed = jnp.zeros((128, HEAD_SIZE), F32)
        for i, piece in enumerate(in_three(top) + in_three(total)):
            packed = jnp.where(lanes == i, piece, packed)
        message = jnp.concatenate(
            [summed.reshape(16, 8, HEAD_SIZE), packed.reshape(16, 8, HEAD_SIZE)], axis=1
        ).astype(BF16)
        for a in range(NEW_TOKENS):
            send5[pl.ds(16 * a + 8 * g, 8)] = message[8 * a : 8 * a + 8]

    for peer in seq_peers:
        scatter_copy(4, send5.at[peer], recv5.at[s], (peer, t)).start()
    pending.append(lambda: await_sent(4, send5, seq - 1))
    recv5[s] = send5[s]

    twin = lax.rem(s, GAME_COUNT * CANDIDATE_MOVES)
    firsts = rows[pl.ds(twin, 1)].astype(F32)[0]
    seconds = rows[pl.ds(twin + 16, 1)].astype(F32)[0]
    score_a = jnp.sum(own_queries * firsts[8:9, :], axis=-1, keepdims=True) * factor
    score_b = jnp.sum(own_queries * seconds[8:9, :], axis=-1, keepdims=True) * factor
    score_b = jnp.where(step >= 1, score_b, FLOOR)
    fresh_top = jnp.maximum(score_a, score_b)
    fresh_a = jnp.exp2(score_a - fresh_top)
    fresh_b = jnp.exp2(score_b - fresh_top)
    fresh_total = fresh_a + fresh_b
    fresh_sum = rounded(fresh_a) * firsts[9:10, :] + rounded(fresh_b) * seconds[9:10, :]
    pick = lax.broadcasted_iota(jnp.int32, (HEAD_SIZE, 2 * HEAD_SIZE), 0)
    side = lax.broadcasted_iota(jnp.int32, (HEAD_SIZE, 2 * HEAD_SIZE), 1) >= HEAD_SIZE
    pick = pick - jnp.where(side, 3, 0)
    picker = jnp.where((pick >= 0) & (pick < 3), 1.0, 0.0).astype(BF16)
    await_all(4, recv5, seq - 1)

    parts = recv5[...].astype(F32)
    unpacked = jnp.dot(
        parts[:, 8:, :].reshape(seq * 8, HEAD_SIZE).astype(BF16),
        picker,
        preferred_element_type=F32,
    )
    tops = unpacked[:, :HEAD_SIZE].reshape(seq, 8, HEAD_SIZE)
    totals = unpacked[:, HEAD_SIZE:].reshape(seq, 8, HEAD_SIZE)
    highest = jnp.maximum(jnp.max(tops, axis=0), fresh_top)
    shares = jnp.exp2(tops - highest[None])
    fresh_share = jnp.exp2(fresh_top - highest)
    whole = jnp.sum(shares * totals, axis=0) + fresh_share * fresh_total
    summed = jnp.sum(shares * parts[:, :8, :], axis=0) + fresh_share * fresh_sum
    context = rounded(summed / whole)
    send6[...] = context
    here = pl.ds(pl.multiple_of(s * 8, 8), 8)
    recv6[here, :] = context

    for peer in seq_peers:
        scatter_copy(5, send6, recv6.at[here], (peer, t)).start()
    pending.append(lambda: await_sent(5, recv6, (seq - 1) * 8))
    need(5)
    await_all(5, recv6, (seq - 1) * 8)

    contexts = jnp.concatenate(
        [recv6[pl.ds(j, ROWS, stride=8), :] for j in range(GROUP)], axis=1
    ).astype(BF16)
    product = jnp.dot(contexts, ow[...], preferred_element_type=F32)
    share = ROWS // 8
    for z in range(8):
        send7[z, 0:share, :] = product[z * share : (z + 1) * share, :HEAD_SIZE]
        send7[z, share : 2 * share, :] = product[z * share : (z + 1) * share, HEAD_SIZE:]

    for peer in tp_peers:
        scatter_copy(6, send7.at[peer], recv7.at[t], (s, peer)).start()
    pending.append(lambda: await_sent(6, send7, tp - 1))
    recv7[t] = send7[t]
    await_all(6, recv7, tp - 1)
    result = jnp.sum(recv7[...], axis=0)
    out[...] = jnp.concatenate([result[:share], result[share:]], axis=1).astype(BF16)

    for wait in pending:
        wait()


def local(
    token_ids,
    lengths,
    norm_gain,
    emb_table,
    q_weight,
    key_matrix,
    value_matrix,
    o_weight,
    key_cache,
    value_cache,
):
    seq, tp = lax.axis_size("seq"), lax.axis_size("tp")
    width = emb_table.shape[1] // seq
    shard_len = key_cache.shape[1]
    vmem, smem, hbm = pltpu.VMEM, pltpu.SMEM, pltpu.HBM
    cache = (GAME_COUNT, shard_len, HEAD_SIZE)
    return pl.pallas_call(
        kernel,
        out_shape=jax.ShapeDtypeStruct((ROWS // tp, width), BF16),
        in_specs=[pl.BlockSpec(memory_space=m) for m in [smem, smem, vmem, vmem] + [hbm] * 7],
        out_specs=pl.BlockSpec(memory_space=vmem),
        scratch_shapes=[
            vmem((seq, emb_table.shape[0], width), BF16),
            vmem(q_weight.shape, BF16),
            vmem(key_matrix.shape, BF16),
            vmem(value_matrix.shape, BF16),
            vmem(o_weight.shape, BF16),
            vmem(cache, BF16),
            vmem(cache, BF16),
            vmem((seq, ROWS, width), BF16),
            vmem((seq, ROWS, width), BF16),
            vmem((ROWS, width), BF16),
            vmem((tp, ROWS, width), BF16),
            vmem((ROWS * 16, HEAD_SIZE), F32),
            vmem((ROWS, 16, HEAD_SIZE), BF16),
            vmem((seq, 16, HEAD_SIZE), BF16),
            vmem((ROWS, 16, HEAD_SIZE), BF16),
            vmem((ROWS, 16, HEAD_SIZE), BF16),
            vmem((seq, 16, HEAD_SIZE), BF16),
            vmem((8, HEAD_SIZE), F32),
            vmem((ROWS * 8, HEAD_SIZE), F32),
            vmem((tp, 8, HEAD_SIZE), F32),
            vmem((tp, 8, HEAD_SIZE), F32),
            pltpu.SemaphoreType.DMA((seq,)),
            pltpu.SemaphoreType.DMA((6,)),
            pltpu.SemaphoreType.DMA((7,)),
            pltpu.SemaphoreType.DMA((7,)),
        ],
        compiler_params=pltpu.CompilerParams(
            collective_id=0, has_side_effects=True, vmem_limit_bytes=60 * 1024 * 1024
        ),
    )(
        token_ids,
        lengths,
        norm_gain,
        jnp.asarray(rotary_rates(HEAD_SIZE)),
        emb_table,
        q_weight,
        key_matrix,
        value_matrix,
        o_weight,
        key_cache.reshape(cache),
        value_cache.reshape(cache),
    )


def solution(mesh):
    placed = (
        P(),
        P(),
        P("seq"),
        P(("seq", "tp"), None),
        P("seq", "tp"),
        P("seq", "tp"),
        P("seq", "tp"),
        P("tp", "seq"),
        P(None, "seq", "tp", None),
        P(None, "seq", "tp", None),
    )
    return jax.shard_map(
        local, mesh=mesh, in_specs=placed, out_specs=P("tp", "seq"), check_vma=False
    )
```

```python
import functools

import jax
import jax.numpy as jnp
import numpy as np
from jax import lax
from jax.experimental import pallas as pl
from jax.experimental.pallas import tpu as pltpu
from jax.sharding import PartitionSpec as P

MODEL_WIDTH = 8192
QUERY_HEADS = 64
KEY_HEADS = 8
HEAD_SIZE = 128
GAME_COUNT = 2
CANDIDATE_MOVES = 8
NEW_TOKENS = 2
ROWS = NEW_TOKENS * GAME_COUNT * CANDIDATE_MOVES
GROUP = QUERY_HEADS // KEY_HEADS

EPSILON = 1e-05
FLOOR = -1e30
LOWEST = -1e29
LOG2E = 1.4426950408889634
SLOTS = 8
GROUP_SLOTS = 16
MESH = pl.DeviceIdType.MESH
F32 = jnp.float32
BF16 = jnp.bfloat16


def rotary_rates(head_dim):
    half_dim = head_dim // 2
    plain_rate = 500000.0 ** (-(np.arange(half_dim) * 2.0) / head_dim)
    wave_len = 2.0 * np.pi / plain_rate
    blend = (8192.0 / wave_len - 1.0) / 3.0
    scaled = np.where(
        wave_len < 2048.0,
        plain_rate,
        np.where(
            wave_len > 8192.0,
            plain_rate / 8.0,
            (1.0 - blend) * plain_rate / 8.0 + blend * plain_rate,
        ),
    )
    return np.concatenate([scaled, scaled]).astype(np.float32).reshape(1, head_dim)


def rounded(x):
    return x.astype(BF16).astype(F32)


def in_three(x):
    high = rounded(x)
    middle = rounded(x - high)
    return high, middle, rounded(x - high - middle)


def kernel(
    compact,
    ids,
    lengths,
    gain,
    rates,
    emb,
    q_weight,
    key_matrix,
    value_matrix,
    o_weight,
    key_cache,
    value_cache,
    out,
    overflow,
    table,
    qw,
    kw,
    vw,
    ow,
    kc,
    vc,
    send1,
    recv1,
    send2,
    recv2,
    spread,
    send3,
    recv3,
    rows,
    send5,
    recv5,
    send6,
    recv6,
    send7,
    recv7,
    table_sems,
    load_sems,
    send_sems,
    recv_sems,
):
    seq, tp = lax.axis_size("seq"), lax.axis_size("tp")
    s, t = lax.axis_index("seq"), lax.axis_index("tp")
    width = gain.shape[0]
    vocab_local = emb.shape[0]
    shard_len = key_cache.shape[1]
    scale = HEAD_SIZE ** (-0.5)

    y, x, core = lax.div(s, 8), lax.rem(lax.div(s, 2), 4), lax.rem(s, 2)

    def moved(dy, dx, dc):
        return (lax.rem(y + dy, 4) * 4 + lax.rem(x + dx, 4)) * 2 + lax.rem(core + dc, 2)

    steps = [(dy, dx, dc) for dy in range(4) for dx in range(4) for dc in range(2)]
    steps.sort(key=lambda d: -10 * (min(d[0], 4 - d[0]) + min(d[1], 4 - d[1])) - d[2])
    seq_peers = [moved(*d) for d in steps[:-1]]
    tp_peers = [lax.rem(t + d, tp) for d in (4, 3, 5, 2, 6, 1, 7)]

    barrier = pltpu.get_barrier_semaphore()

    for device in [(peer, t) for peer in seq_peers] + [(s, peer) for peer in tp_peers]:
        pl.semaphore_signal(barrier, inc=1, device_id=device, device_id_type=MESH)

    planes = [lax.rem(y + dy, 4) for dy in (2, 1, 3, 0)]
    stripe = table.shape[2]
    table_loads = [
        pltpu.make_async_copy(
            emb.at[:, pl.ds(pl.multiple_of(plane * stripe, stripe), stripe)],
            table.at[i],
            table_sems.at[i],
        )
        for i, plane in enumerate(planes)
    ]
    for load in table_loads:
        load.start()
    loads = [
        pltpu.make_async_copy(src, dst, load_sems.at[i])
        for i, (src, dst) in enumerate(
            [
                (q_weight, qw),
                (key_matrix, kw),
                (value_matrix, vw),
                (key_cache, kc),
                (value_cache, vc),
                (o_weight, ow),
            ]
        )
    ]
    pending, loaded = [], set()

    def need(*names):
        for i in names:
            loads[i].wait()
            loaded.add(i)

    tokens = [ids[r // 16, (r // 8) % 2, r % 8] for r in range(ROWS)]
    down = jnp.zeros((ROWS, HEAD_SIZE), jnp.int32)
    along = jnp.zeros((ROWS, HEAD_SIZE), jnp.int32)
    rows_at = lax.broadcasted_iota(jnp.int32, (ROWS, HEAD_SIZE), 0)
    lanes_at = lax.broadcasted_iota(jnp.int32, (ROWS, HEAD_SIZE), 1)
    for r, token in enumerate(tokens):
        down = jnp.where(rows_at == r, token, down)
        along = jnp.where(lanes_at == r, token, along)
    in_block = vocab_local.bit_length() - 1
    block_down, block_along = jnp.right_shift(down, in_block), jnp.right_shift(along, in_block)
    plane_down, plane_along = block_down & (tp - 1), block_along & (tp - 1)
    first_id = (s * tp + t) * vocab_local
    token_rows = jnp.concatenate([down - first_id] * (vocab_local // HEAD_SIZE), axis=1)
    hits = jnp.where(
        token_rows == lax.broadcasted_iota(jnp.int32, (ROWS, vocab_local), 1), 1.0, 0.0
    ).astype(BF16)
    if compact:
        earlier, later = (lanes_at < rows_at), (rows_at < lanes_at)

        def slots(there, here):
            same = there == here
            by_row = jnp.sum(jnp.where(same & earlier, 1.0, 0.0), axis=1, keepdims=True)
            by_lane = jnp.sum(jnp.where(same & later, 1.0, 0.0), axis=0, keepdims=True)
            return by_row.astype(jnp.int32), by_lane.astype(jnp.int32)

        slot_down, slot_along = slots(block_down, block_along)
        group_down, group_along = slots(plane_down, plane_along)
        too_many = (jnp.max(slot_down) >= SLOTS) | (jnp.max(group_down) >= GROUP_SLOTS)
        overflow[0] = jnp.where(too_many, 1, 0)
        token_lane = lanes_at < ROWS
        mine = (block_along == s * tp + t) & (slot_along == rows_at) & token_lane
        mine = jnp.where(mine, 1.0, 0.0).astype(BF16)[:16, :ROWS]
        one_hot = jnp.dot(mine, hits, preferred_element_type=F32).astype(BF16)
        ours = (plane_along == t) & (group_along == rows_at) & token_lane
        ours = jnp.where(ours, 1.0, 0.0).astype(BF16)[:GROUP_SLOTS, :ROWS]
        spot = jnp.right_shift(block_down[:, :1], tp.bit_length() - 1) * 16 + slot_down
        spots = lax.broadcasted_iota(jnp.int32, (ROWS, seq * 16), 1)
        to_group = jnp.concatenate(
            [
                jnp.dot(
                    ours,
                    jnp.where(spots == spot + half * SLOTS, 1.0, 0.0).astype(BF16),
                    preferred_element_type=F32,
                )
                for half in range(2)
            ],
            axis=0,
        ).astype(BF16)
        spot = plane_down[:, :1] * GROUP_SLOTS + group_down
        to_rows = jnp.where(
            lax.broadcasted_iota(jnp.int32, (ROWS, tp * GROUP_SLOTS), 1) == spot, 1.0, 0.0
        ).astype(BF16)
    else:
        overflow[0] = 0
        one_hot = hits

    for i, plane in enumerate(planes):
        table_loads[i].wait()
        found = jnp.dot(one_hot, table[i], preferred_element_type=F32)
        for j in range(stripe // width):
            part = found[:, j * width : (j + 1) * width]
            if compact:
                part = jnp.concatenate(
                    [part[:SLOTS, :HEAD_SIZE], part[:SLOTS, HEAD_SIZE:]], axis=0
                )
            send1[plane * (stripe // width) + j] = part.astype(BF16)

    def scatter_copy(phase, source, target, device):
        return pltpu.make_async_remote_copy(
            src_ref=source,
            dst_ref=target,
            send_sem=send_sems.at[phase],
            recv_sem=recv_sems.at[phase],
            device_id=device,
            device_id_type=MESH,
        )

    def await_all(phase, buffer, count):
        part = buffer.at[pl.ds(0, count)]
        pltpu.make_async_copy(part, part, recv_sems.at[phase]).wait()

    def await_sent(phase, buffer, count):
        part = buffer.at[pl.ds(0, count)]
        pltpu.make_async_copy(part, part, send_sems.at[phase]).wait()

    pl.semaphore_wait(barrier, seq + tp - 2)

    for peer in seq_peers:
        scatter_copy(0, send1.at[peer], recv1.at[s], (peer, t)).start()
    pending.append(lambda: await_sent(0, send1, seq - 1))
    recv1[s] = send1[s]
    for load in loads:
        load.start()
    await_all(0, recv1, seq - 1)

    if compact:
        found = jnp.dot(
            to_group, recv1[...].reshape(seq * 16, HEAD_SIZE), preferred_element_type=F32
        )
        found = jnp.concatenate([found[:GROUP_SLOTS], found[GROUP_SLOTS:]], axis=1).astype(BF16)
    else:
        found = jnp.sum(recv1[...].astype(F32), axis=0).astype(BF16)
    send2[...] = found
    for peer in tp_peers:
        scatter_copy(1, send2, recv2.at[t], (s, peer)).start()
    pending.append(lambda: await_sent(1, recv2, tp - 1))
    recv2[t] = found
    await_all(1, recv2, tp - 1)
    if compact:
        embedded = jnp.dot(
            to_rows, recv2[...].reshape(tp * GROUP_SLOTS, width), preferred_element_type=F32
        )
    else:
        embedded = jnp.sum(recv2[...].astype(F32), axis=0)

    squares = jnp.sum(embedded * embedded, axis=-1, keepdims=True)
    normed = (embedded * gain[...].astype(F32)[None, :]).astype(BF16)
    need(0, 1, 2)
    query_part = jnp.dot(normed, qw[...], preferred_element_type=F32)
    key_part = jnp.dot(normed, kw[...], preferred_element_type=F32)
    value_part = jnp.dot(normed, vw[...], preferred_element_type=F32)
    for j in range(GROUP):
        spread[pl.ds(j, ROWS, stride=16), :] = query_part[:, j * HEAD_SIZE : (j + 1) * HEAD_SIZE]
    spread[pl.ds(8, ROWS, stride=16), :] = key_part
    spread[pl.ds(9, ROWS, stride=16), :] = value_part
    for j in range(10, 16):
        spread[pl.ds(j, ROWS, stride=16), :] = jnp.broadcast_to(squares, (ROWS, HEAD_SIZE))
    send3[...] = spread[...].reshape(ROWS, 16, HEAD_SIZE).astype(BF16)

    for peer in seq_peers:
        scatter_copy(2, send3.at[peer], recv3.at[s], (peer, t)).start()
    pending.append(lambda: await_sent(2, send3, seq - 1))
    recv3[s] = send3[s]
    game = lax.rem(lax.div(s, CANDIDATE_MOVES), GAME_COUNT)
    step = lax.div(s, GAME_COUNT * CANDIDATE_MOVES)
    position = (lengths[game] + step).astype(F32)
    angles = position * rates[...]
    lane = lax.broadcasted_iota(jnp.int32, (1, HEAD_SIZE), 1)
    cosine = jnp.cos(angles)
    sine = jnp.sin(angles)
    sine = jnp.where(lane < HEAD_SIZE // 2, -sine, sine)
    await_all(2, recv3, seq - 1)

    sums = jnp.sum(recv3[...].astype(F32), axis=0)
    inv_rms = lax.rsqrt(sums[10:11, :] / MODEL_WIDTH + EPSILON)
    scaled = sums * inv_rms
    turned = scaled * cosine + pltpu.roll(scaled, HEAD_SIZE // 2, 1) * sine
    place = lax.broadcasted_iota(jnp.int32, (16, HEAD_SIZE), 0)
    own = jnp.where(place < 9, turned, scaled).astype(BF16)
    rows[s] = own

    for peer in seq_peers:
        scatter_copy(3, rows.at[s], rows.at[s], (peer, t)).start()
    pending.append(lambda: await_sent(3, rows, seq - 1))
    own_queries = own.astype(F32)[:8, :]
    need(3, 4)
    await_all(3, rows, seq - 1)

    factor = scale * LOG2E
    for g in range(GAME_COUNT):
        halves = [
            rows[pl.ds(16 * a + 8 * g, 8)].astype(F32)[:, :8, :].reshape(64, HEAD_SIZE)
            for a in range(NEW_TOKENS)
        ]
        queries = jnp.concatenate(halves, axis=0).astype(BF16)
        scores = lax.dot_general(
            queries, kc[g], (((1,), (1,)), ((), ())), preferred_element_type=F32
        )
        slot = s * shard_len + lax.broadcasted_iota(jnp.int32, (1, shard_len), 1)
        masked = jnp.where(slot < lengths[g], scores * factor, FLOOR)
        top = jnp.maximum(jnp.max(masked, axis=-1, keepdims=True), LOWEST)
        shifted = jnp.exp2(masked - top)
        total = jnp.sum(shifted, axis=-1, keepdims=True)
        summed = jnp.dot(shifted.astype(BF16), vc[g], preferred_element_type=F32)
        lanes = lax.broadcasted_iota(jnp.int32, (128, HEAD_SIZE), 1)
        packed = jnp.zeros((128, HEAD_SIZE), F32)
        for i, piece in enumerate(in_three(top) + in_three(total)):
            packed = jnp.where(lanes == i, piece, packed)
        message = jnp.concatenate(
            [summed.reshape(16, 8, HEAD_SIZE), packed.reshape(16, 8, HEAD_SIZE)], axis=1
        ).astype(BF16)
        for a in range(NEW_TOKENS):
            send5[pl.ds(16 * a + 8 * g, 8)] = message[8 * a : 8 * a + 8]

    for peer in seq_peers:
        scatter_copy(4, send5.at[peer], recv5.at[s], (peer, t)).start()
    pending.append(lambda: await_sent(4, send5, seq - 1))
    recv5[s] = send5[s]

    twin = lax.rem(s, GAME_COUNT * CANDIDATE_MOVES)
    firsts = rows[pl.ds(twin, 1)].astype(F32)[0]
    seconds = rows[pl.ds(twin + 16, 1)].astype(F32)[0]
    score_a = jnp.sum(own_queries * firsts[8:9, :], axis=-1, keepdims=True) * factor
    score_b = jnp.sum(own_queries * seconds[8:9, :], axis=-1, keepdims=True) * factor
    score_b = jnp.where(step >= 1, score_b, FLOOR)
    fresh_top = jnp.maximum(score_a, score_b)
    fresh_a = jnp.exp2(score_a - fresh_top)
    fresh_b = jnp.exp2(score_b - fresh_top)
    fresh_total = fresh_a + fresh_b
    fresh_sum = rounded(fresh_a) * firsts[9:10, :] + rounded(fresh_b) * seconds[9:10, :]
    pick = lax.broadcasted_iota(jnp.int32, (HEAD_SIZE, 2 * HEAD_SIZE), 0)
    side = lax.broadcasted_iota(jnp.int32, (HEAD_SIZE, 2 * HEAD_SIZE), 1) >= HEAD_SIZE
    pick = pick - jnp.where(side, 3, 0)
    picker = jnp.where((pick >= 0) & (pick < 3), 1.0, 0.0).astype(BF16)
    await_all(4, recv5, seq - 1)

    parts = recv5[...].astype(F32)
    unpacked = jnp.dot(
        parts[:, 8:, :].reshape(seq * 8, HEAD_SIZE).astype(BF16),
        picker,
        preferred_element_type=F32,
    )
    tops = unpacked[:, :HEAD_SIZE].reshape(seq, 8, HEAD_SIZE)
    totals = unpacked[:, HEAD_SIZE:].reshape(seq, 8, HEAD_SIZE)
    highest = jnp.maximum(jnp.max(tops, axis=0), fresh_top)
    shares = jnp.exp2(tops - highest[None])
    fresh_share = jnp.exp2(fresh_top - highest)
    whole = jnp.sum(shares * totals, axis=0) + fresh_share * fresh_total
    summed = jnp.sum(shares * parts[:, :8, :], axis=0) + fresh_share * fresh_sum
    context = rounded(summed / whole)
    send6[...] = context
    here = pl.ds(pl.multiple_of(s * 8, 8), 8)
    recv6[here, :] = context

    for peer in seq_peers:
        scatter_copy(5, send6, recv6.at[here], (peer, t)).start()
    pending.append(lambda: await_sent(5, recv6, (seq - 1) * 8))
    need(5)
    await_all(5, recv6, (seq - 1) * 8)

    contexts = jnp.concatenate(
        [recv6[pl.ds(j, ROWS, stride=8), :] for j in range(GROUP)], axis=1
    ).astype(BF16)
    product = jnp.dot(contexts, ow[...], preferred_element_type=F32)
    share = ROWS // 8
    for z in range(8):
        send7[z, 0:share, :] = product[z * share : (z + 1) * share, :HEAD_SIZE]
        send7[z, share : 2 * share, :] = product[z * share : (z + 1) * share, HEAD_SIZE:]

    for peer in tp_peers:
        scatter_copy(6, send7.at[peer], recv7.at[t], (s, peer)).start()
    pending.append(lambda: await_sent(6, send7, tp - 1))
    recv7[t] = send7[t]
    await_all(6, recv7, tp - 1)
    result = jnp.sum(recv7[...], axis=0)
    out[...] = jnp.concatenate([result[:share], result[share:]], axis=1).astype(BF16)

    for wait in pending:
        wait()


def local(
    token_ids,
    lengths,
    norm_gain,
    emb_table,
    q_weight,
    key_matrix,
    value_matrix,
    o_weight,
    key_cache,
    value_cache,
):
    seq, tp = lax.axis_size("seq"), lax.axis_size("tp")
    width = emb_table.shape[1] // seq
    cache = (GAME_COUNT, key_cache.shape[1], HEAD_SIZE)
    vmem, smem, hbm = pltpu.VMEM, pltpu.SMEM, pltpu.HBM
    operands = (
        token_ids,
        lengths,
        norm_gain,
        jnp.asarray(rotary_rates(HEAD_SIZE)),
        emb_table,
        q_weight,
        key_matrix,
        value_matrix,
        o_weight,
        key_cache.reshape(cache),
        value_cache.reshape(cache),
    )

    def run(compact):
        row_message = (16, HEAD_SIZE) if compact else (ROWS, width)
        group_message = (GROUP_SLOTS, width) if compact else (ROWS, width)
        return pl.pallas_call(
            functools.partial(kernel, compact),
            out_shape=(
                jax.ShapeDtypeStruct((ROWS // tp, width), BF16),
                jax.ShapeDtypeStruct((1,), jnp.int32),
            ),
            in_specs=[pl.BlockSpec(memory_space=m) for m in [smem, smem, vmem, vmem] + [hbm] * 7],
            out_specs=(pl.BlockSpec(memory_space=vmem), pl.BlockSpec(memory_space=smem)),
            scratch_shapes=[
                vmem((4, emb_table.shape[0], emb_table.shape[1] // 4), BF16),
                vmem(q_weight.shape, BF16),
                vmem(key_matrix.shape, BF16),
                vmem(value_matrix.shape, BF16),
                vmem(o_weight.shape, BF16),
                vmem(cache, BF16),
                vmem(cache, BF16),
                vmem((seq,) + row_message, BF16),
                vmem((seq,) + row_message, BF16),
                vmem(group_message, BF16),
                vmem((tp,) + group_message, BF16),
                vmem((ROWS * 16, HEAD_SIZE), F32),
                vmem((ROWS, 16, HEAD_SIZE), BF16),
                vmem((seq, 16, HEAD_SIZE), BF16),
                vmem((ROWS, 16, HEAD_SIZE), BF16),
                vmem((ROWS, 16, HEAD_SIZE), BF16),
                vmem((seq, 16, HEAD_SIZE), BF16),
                vmem((8, HEAD_SIZE), F32),
                vmem((ROWS * 8, HEAD_SIZE), F32),
                vmem((tp, 8, HEAD_SIZE), F32),
                vmem((tp, 8, HEAD_SIZE), F32),
                pltpu.SemaphoreType.DMA((4,)),
                pltpu.SemaphoreType.DMA((6,)),
                pltpu.SemaphoreType.DMA((7,)),
                pltpu.SemaphoreType.DMA((7,)),
            ],
            compiler_params=pltpu.CompilerParams(
                collective_id=0 if compact else 1,
                has_side_effects=True,
                vmem_limit_bytes=64 * 1024 * 1024,
            ),
        )(*operands)

    result, overflow = run(True)
    return lax.cond(overflow[0] > 0, lambda: run(False)[0], lambda: result)


def solution(mesh):
    placed = (
        P(),
        P(),
        P("seq"),
        P(("seq", "tp"), None),
        P("seq", "tp"),
        P("seq", "tp"),
        P("seq", "tp"),
        P("tp", "seq"),
        P(None, "seq", "tp", None),
        P(None, "seq", "tp", None),
    )
    return jax.shard_map(
        local, mesh=mesh, in_specs=placed, out_specs=P("tp", "seq"), check_vma=False
    )
```

```python
import functools

import jax
import jax.numpy as jnp
import numpy as np
from jax import lax
from jax.experimental import pallas as pl
from jax.experimental.pallas import tpu as pltpu
from jax.sharding import PartitionSpec as P

MODEL_WIDTH = 8192
QUERY_HEADS = 64
KEY_HEADS = 8
HEAD_SIZE = 128
GAME_COUNT = 2
CANDIDATE_MOVES = 8
NEW_TOKENS = 2
ROWS = NEW_TOKENS * GAME_COUNT * CANDIDATE_MOVES
GROUP = QUERY_HEADS // KEY_HEADS

EPSILON = 1e-05
FLOOR = -1e30
LOWEST = -1e29
LOG2E = 1.4426950408889634
SLOTS = 4
GROUP_SLOTS = 12
KEYS = 1024
MESH = pl.DeviceIdType.MESH
F32 = jnp.float32
BF16 = jnp.bfloat16


def rotary_rates(head_dim):
    half_dim = head_dim // 2
    plain_rate = 500000.0 ** (-(np.arange(half_dim) * 2.0) / head_dim)
    wave_len = 2.0 * np.pi / plain_rate
    blend = (8192.0 / wave_len - 1.0) / 3.0
    scaled = np.where(
        wave_len < 2048.0,
        plain_rate,
        np.where(
            wave_len > 8192.0,
            plain_rate / 8.0,
            (1.0 - blend) * plain_rate / 8.0 + blend * plain_rate,
        ),
    )
    return np.concatenate([scaled, scaled]).astype(np.float32).reshape(1, head_dim)


def rounded(x):
    return x.astype(BF16).astype(F32)


def in_three(x):
    high = rounded(x)
    middle = rounded(x - high)
    return high, middle, rounded(x - high - middle)


def kernel(
    compact,
    ids,
    lengths,
    gain,
    rates,
    emb,
    q_weight,
    key_matrix,
    value_matrix,
    o_weight,
    key_cache,
    value_cache,
    out,
    overflow,
    table,
    weights,
    ow,
    kc,
    vc,
    send1,
    recv1,
    send2,
    recv2,
    spread,
    send3,
    recv3,
    rows,
    pair,
    scores,
    send5,
    recv5,
    recv6,
    wide,
    send7,
    recv7,
    table_sems,
    load_sems,
    send_sems,
    recv_sems,
):
    seq, tp = lax.axis_size("seq"), lax.axis_size("tp")
    s, t = lax.axis_index("seq"), lax.axis_index("tp")
    width = gain.shape[0]
    vocab_local = emb.shape[0]
    heads = q_weight.shape[1]
    shard_len = key_cache.shape[1]
    scale = HEAD_SIZE ** (-0.5)

    y, x, core = lax.div(s, 8), lax.rem(lax.div(s, 2), 4), lax.rem(s, 2)

    def moved(dy, dx, dc):
        return (lax.rem(y + dy, 4) * 4 + lax.rem(x + dx, 4)) * 2 + lax.rem(core + dc, 2)

    steps = [(dy, dx, dc) for dy in range(4) for dx in range(4) for dc in range(2)]
    steps.sort(key=lambda d: -10 * (min(d[0], 4 - d[0]) + min(d[1], 4 - d[1])) - d[2])
    seq_peers = [moved(*d) for d in steps[:-1]]
    tp_peers = [lax.rem(t + d, tp) for d in (4, 3, 5, 2, 6, 1, 7)]

    planes = [lax.rem(y + dy, 4) for dy in (2, 1, 3, 0)]
    stripe = table.shape[2]
    table_loads = [
        pltpu.make_async_copy(
            emb.at[:, pl.ds(pl.multiple_of(plane * stripe, stripe), stripe)],
            table.at[i],
            table_sems.at[i],
        )
        for i, plane in enumerate(planes)
    ]
    for load in table_loads:
        load.start()

    barrier = pltpu.get_barrier_semaphore()

    greeted = [(s, peer) for peer in tp_peers]
    greeted = greeted[:3] + [(peer, t) for peer in seq_peers[:22]] + greeted[3:]
    for device in greeted + [(peer, t) for peer in seq_peers[22:]]:
        pl.semaphore_signal(barrier, inc=1, device_id=device, device_id_type=MESH)

    loads = [
        pltpu.make_async_copy(src, dst, load_sems.at[i])
        for i, (src, dst) in enumerate(
            [
                (q_weight, weights.at[:, pl.ds(0, heads)]),
                (key_matrix, weights.at[:, pl.ds(heads, HEAD_SIZE)]),
                (value_matrix, weights.at[:, pl.ds(heads + HEAD_SIZE, HEAD_SIZE)]),
                (key_cache, kc),
                (value_cache, vc.at[:, :, pl.ds(0, HEAD_SIZE)]),
                (o_weight, ow),
            ]
        )
    ]
    pending, loaded = [], set()

    def need(*names):
        for i in names:
            loads[i].wait()
            loaded.add(i)

    tokens = [ids[r // 16, (r // 8) % 2, r % 8] for r in range(ROWS)]
    down = jnp.zeros((ROWS, HEAD_SIZE), jnp.int32)
    along = jnp.zeros((ROWS, HEAD_SIZE), jnp.int32)
    rows_at = lax.broadcasted_iota(jnp.int32, (ROWS, HEAD_SIZE), 0)
    lanes_at = lax.broadcasted_iota(jnp.int32, (ROWS, HEAD_SIZE), 1)
    for r, token in enumerate(tokens):
        down = jnp.where(rows_at == r, token, down)
        along = jnp.where(lanes_at == r, token, along)
    in_block = vocab_local.bit_length() - 1
    block_down, block_along = jnp.right_shift(down, in_block), jnp.right_shift(along, in_block)
    plane_down, plane_along = block_down & (tp - 1), block_along & (tp - 1)
    first_id = (s * tp + t) * vocab_local
    token_rows = jnp.concatenate([down - first_id] * (vocab_local // HEAD_SIZE), axis=1)
    hits = jnp.where(
        token_rows == lax.broadcasted_iota(jnp.int32, (ROWS, vocab_local), 1), 1.0, 0.0
    ).astype(BF16)
    if compact:
        earlier, later = (lanes_at < rows_at), (rows_at < lanes_at)

        def slots(there, here):
            same = there == here
            by_row = jnp.sum(jnp.where(same & earlier, 1.0, 0.0), axis=1, keepdims=True)
            by_lane = jnp.sum(jnp.where(same & later, 1.0, 0.0), axis=0, keepdims=True)
            return by_row.astype(jnp.int32), by_lane.astype(jnp.int32)

        slot_down, slot_along = slots(block_down, block_along)
        group_down, group_along = slots(plane_down, plane_along)
        too_many = (jnp.max(slot_down) >= SLOTS) | (jnp.max(group_down) >= GROUP_SLOTS)
        overflow[0] = jnp.where(too_many, 1, 0)
        token_lane = lanes_at < ROWS
        mine = (block_along == s * tp + t) & (slot_along == rows_at) & token_lane
        mine = jnp.where(mine, 1.0, 0.0).astype(BF16)[:16, :ROWS]
        one_hot = jnp.dot(mine, hits, preferred_element_type=F32).astype(BF16)
        ours = (plane_along == t) & (group_along == rows_at) & token_lane
        ours = jnp.where(ours, 1.0, 0.0).astype(BF16)[:16, :ROWS]
        spot = jnp.right_shift(block_down[:, :1], tp.bit_length() - 1) * 2 * SLOTS + slot_down
        spots = lax.broadcasted_iota(jnp.int32, (ROWS, seq * 2 * SLOTS), 1)
        to_group = jnp.concatenate(
            [
                jnp.dot(
                    ours,
                    jnp.where(spots == spot + half * SLOTS, 1.0, 0.0).astype(BF16),
                    preferred_element_type=F32,
                )[:GROUP_SLOTS]
                for half in range(2)
            ],
            axis=0,
        ).astype(BF16)
        spot = plane_down[:, :1] * 2 * GROUP_SLOTS + group_down
        spots = lax.broadcasted_iota(jnp.int32, (ROWS, tp * 2 * GROUP_SLOTS), 1)
        to_rows = jnp.concatenate(
            [jnp.where(spots == spot + half * GROUP_SLOTS, 1.0, 0.0) for half in range(2)], axis=0
        ).astype(BF16)
    else:
        overflow[0] = 0
        one_hot = hits

    for i, plane in enumerate(planes):
        table_loads[i].wait()
        found = jnp.dot(one_hot, table[i], preferred_element_type=F32)
        for j in range(stripe // width):
            part = found[:, j * width : (j + 1) * width]
            if compact:
                part = jnp.concatenate(
                    [part[:SLOTS, :HEAD_SIZE], part[:SLOTS, HEAD_SIZE:]], axis=0
                )
            send1[plane * (stripe // width) + j] = part.astype(BF16)

    def scatter_copy(phase, source, target, device):
        return pltpu.make_async_remote_copy(
            src_ref=source,
            dst_ref=target,
            send_sem=send_sems.at[phase],
            recv_sem=recv_sems.at[phase],
            device_id=device,
            device_id_type=MESH,
        )

    def await_all(phase, buffer, count):
        part = buffer.at[pl.ds(0, count)]
        pltpu.make_async_copy(part, part, recv_sems.at[phase]).wait()

    def await_sent(phase, buffer, count):
        part = buffer.at[pl.ds(0, count)]
        pltpu.make_async_copy(part, part, send_sems.at[phase]).wait()

    pl.semaphore_wait(barrier, seq + tp - 2)

    for peer in seq_peers:
        scatter_copy(0, send1.at[peer], recv1.at[s], (peer, t)).start()
    pending.append(lambda: await_sent(0, send1, seq - 1))
    recv1[s] = send1[s]
    for load in loads:
        load.start()
    vc[:, :, HEAD_SIZE:] = jnp.ones((GAME_COUNT, shard_len, HEAD_SIZE), BF16)
    await_all(0, recv1, seq - 1)

    if compact:
        arrived = recv1[...].astype(F32).reshape(seq * 2 * SLOTS, HEAD_SIZE).astype(BF16)
        found = jnp.dot(to_group, arrived, preferred_element_type=F32).astype(BF16)
    else:
        found = jnp.sum(recv1[...].astype(F32), axis=0).astype(BF16)
    send2[...] = found
    for peer in tp_peers:
        scatter_copy(1, send2, recv2.at[t], (s, peer)).start()
    pending.append(lambda: await_sent(1, recv2, tp - 1))
    recv2[t] = found
    await_all(1, recv2, tp - 1)
    if compact:
        arrived = recv2[...].astype(F32).reshape(tp * 2 * GROUP_SLOTS, HEAD_SIZE).astype(BF16)
        embedded = jnp.dot(to_rows, arrived, preferred_element_type=F32)
        embedded = jnp.concatenate([embedded[:ROWS], embedded[ROWS:]], axis=1)
    else:
        embedded = jnp.sum(recv2[...].astype(F32), axis=0)

    squares = jnp.sum(embedded * embedded, axis=-1, keepdims=True)
    normed = (embedded * gain[...].astype(F32)[None, :]).astype(BF16)
    need(0, 1, 2)
    products = jnp.dot(normed, weights[...], preferred_element_type=F32)
    for j in range(GROUP + 2):
        spread[pl.ds(j, ROWS, stride=16), :] = products[:, j * HEAD_SIZE : (j + 1) * HEAD_SIZE]
    for j in range(10, 16):
        spread[pl.ds(j, ROWS, stride=16), :] = jnp.broadcast_to(squares, (ROWS, HEAD_SIZE))
    send3[...] = spread[...].reshape(ROWS, 16, HEAD_SIZE).astype(BF16)

    for peer in seq_peers:
        scatter_copy(2, send3.at[peer], recv3.at[s], (peer, t)).start()
    pending.append(lambda: await_sent(2, send3, seq - 1))
    recv3[s] = send3[s]
    game = lax.rem(lax.div(s, CANDIDATE_MOVES), GAME_COUNT)
    step = lax.div(s, GAME_COUNT * CANDIDATE_MOVES)
    position = (lengths[game] + step).astype(F32)
    angles = position * rates[...]
    lane = lax.broadcasted_iota(jnp.int32, (1, HEAD_SIZE), 1)
    cosine = jnp.cos(angles)
    sine = jnp.sin(angles)
    sine = jnp.where(lane < HEAD_SIZE // 2, -sine, sine)
    await_all(2, recv3, seq - 1)

    sums = jnp.sum(recv3[...].astype(F32), axis=0)
    inv_rms = lax.rsqrt(sums[10:11, :] / MODEL_WIDTH + EPSILON)
    scaled = sums * inv_rms
    turned = scaled * cosine + pltpu.roll(scaled, HEAD_SIZE // 2, 1) * sine
    place = lax.broadcasted_iota(jnp.int32, (16, HEAD_SIZE), 0)
    own = rounded(jnp.where(place < 9, turned, scaled))
    own_queries, own_pair = own[:8], own[8:]
    rows[s] = own_queries.astype(BF16)
    for peer in seq_peers:
        scatter_copy(3, rows.at[s], rows.at[s], (peer, t)).start()
    pending.append(lambda: await_sent(3, rows, seq - 1))
    pair[0] = own_pair
    twin = lax.rem(s + GAME_COUNT * CANDIDATE_MOVES, seq)
    twin_copy = scatter_copy(7, pair.at[0], pair.at[1], (twin, t))
    twin_copy.start()
    need(3, 4)
    await_all(3, rows, seq - 1)

    factor = scale * LOG2E
    games = range(GAME_COUNT)
    chunks = [pl.ds(i, KEYS) for i in range(0, shard_len, KEYS)]
    queries, peaks, tops, sums = [], [], [], []
    for g in games:
        halves = [
            rows[pl.ds(16 * a + 8 * g, 8)].astype(F32).reshape(64, HEAD_SIZE)
            for a in range(NEW_TOKENS)
        ]
        queries.append(jnp.concatenate(halves, axis=0).astype(BF16))
        peaks.append(jnp.full((128, HEAD_SIZE), FLOOR, F32))
    for chunk in chunks:
        slot = s * shard_len + chunk.start + lax.broadcasted_iota(jnp.int32, (1, KEYS), 1)
        for g in games:
            part = lax.dot_general(
                queries[g], kc[g, chunk, :], (((1,), (1,)), ((), ())), preferred_element_type=F32
            )
            part = jnp.where(slot < lengths[g], part, FLOOR)
            scores[g, :, chunk] = part
            for i in range(0, KEYS, HEAD_SIZE):
                peaks[g] = jnp.maximum(peaks[g], part[:, i : i + HEAD_SIZE])
    for g in games:
        tops.append(jnp.maximum(jnp.max(peaks[g], axis=-1, keepdims=True), LOWEST))
        sums.append(jnp.zeros((128, 2 * HEAD_SIZE), F32))
    for chunk in chunks:
        for g in games:
            shifted = jnp.exp2((scores[g, :, chunk] - tops[g]) * factor).astype(BF16)
            sums[g] += jnp.dot(shifted, vc[g, chunk, :], preferred_element_type=F32)
    lanes = lax.broadcasted_iota(jnp.int32, (128, HEAD_SIZE), 1)
    for g in games:
        top = jnp.broadcast_to(tops[g] * factor, (128, HEAD_SIZE))
        high, middle, low = in_three(jnp.where(lanes < 3, top, sums[g][:, HEAD_SIZE:]))
        turn = jnp.where(lanes < 3, lanes, lanes - 3)
        packed = jnp.where(turn == 0, high, jnp.where(turn == 1, middle, low))
        message = jnp.concatenate(
            [sums[g][:, :HEAD_SIZE].reshape(16, 8, HEAD_SIZE), packed.reshape(16, 8, HEAD_SIZE)],
            axis=1,
        ).astype(BF16)
        for a in range(NEW_TOKENS):
            send5[pl.ds(16 * a + 8 * g, 8)] = message[8 * a : 8 * a + 8]
    for peer in seq_peers:
        scatter_copy(4, send5.at[peer], recv5.at[s], (peer, t)).start()
    pending.append(lambda: await_sent(4, send5, seq - 1))
    recv5[s] = send5[s]

    twin_copy.wait()
    firsts = jnp.where(step >= 1, pair[1], own_pair)
    seconds = own_pair
    score_a = jnp.sum(own_queries * firsts[0:1, :], axis=-1, keepdims=True) * factor
    score_b = jnp.sum(own_queries * seconds[0:1, :], axis=-1, keepdims=True) * factor
    score_b = jnp.where(step >= 1, score_b, FLOOR)
    fresh_top = jnp.maximum(score_a, score_b)
    fresh_a = jnp.exp2(score_a - fresh_top)
    fresh_b = jnp.exp2(score_b - fresh_top)
    fresh_total = fresh_a + fresh_b
    fresh_sum = rounded(fresh_a) * firsts[1:2, :] + rounded(fresh_b) * seconds[1:2, :]
    pick = lax.broadcasted_iota(jnp.int32, (HEAD_SIZE, 2 * HEAD_SIZE), 0)
    side = lax.broadcasted_iota(jnp.int32, (HEAD_SIZE, 2 * HEAD_SIZE), 1) >= HEAD_SIZE
    pick = pick - jnp.where(side, 3, 0)
    picker = jnp.where((pick >= 0) & (pick < 3), 1.0, 0.0).astype(BF16)
    await_all(4, recv5, seq - 1)

    parts = recv5[...].astype(F32)
    unpacked = jnp.dot(
        parts[:, 8:, :].reshape(seq * 8, HEAD_SIZE).astype(BF16),
        picker,
        preferred_element_type=F32,
    )
    tops = unpacked[:, :HEAD_SIZE].reshape(seq, 8, HEAD_SIZE)
    totals = unpacked[:, HEAD_SIZE:].reshape(seq, 8, HEAD_SIZE)
    highest = jnp.maximum(jnp.max(tops, axis=0), fresh_top)
    shares = jnp.exp2(tops - highest[None])
    fresh_share = jnp.exp2(fresh_top - highest)
    whole = jnp.sum(shares * totals, axis=0) + fresh_share * fresh_total
    summed = jnp.sum(shares * parts[:, :8, :], axis=0) + fresh_share * fresh_sum
    recv6[s] = (summed / whole).astype(BF16)
    for peer in seq_peers:
        scatter_copy(5, recv6.at[s], recv6.at[s], (peer, t)).start()
    pending.append(lambda: await_sent(5, recv6, seq - 1))
    need(5)
    await_all(5, recv6, seq - 1)

    wide[...] = recv6[...].astype(F32).reshape(ROWS * 8, HEAD_SIZE)
    contexts = jnp.concatenate(
        [wide[pl.ds(j, ROWS, stride=8), :] for j in range(GROUP)], axis=1
    ).astype(BF16)
    product = jnp.dot(contexts, ow[...], preferred_element_type=F32)
    share = ROWS // 8
    for z in range(8):
        send7[z, 0:share, :] = product[z * share : (z + 1) * share, :HEAD_SIZE]
        send7[z, share : 2 * share, :] = product[z * share : (z + 1) * share, HEAD_SIZE:]

    for peer in tp_peers:
        scatter_copy(6, send7.at[peer], recv7.at[t], (s, peer)).start()
    pending.append(lambda: await_sent(6, send7, tp - 1))
    recv7[t] = send7[t]
    await_all(6, recv7, tp - 1)
    result = jnp.sum(recv7[...], axis=0)
    out[...] = jnp.concatenate([result[:share], result[share:]], axis=1).astype(BF16)

    for wait in pending:
        wait()


def local(
    token_ids,
    lengths,
    norm_gain,
    emb_table,
    q_weight,
    key_matrix,
    value_matrix,
    o_weight,
    key_cache,
    value_cache,
):
    seq, tp = lax.axis_size("seq"), lax.axis_size("tp")
    width = emb_table.shape[1] // seq
    cache = (GAME_COUNT, key_cache.shape[1], HEAD_SIZE)
    vmem, smem, hbm = pltpu.VMEM, pltpu.SMEM, pltpu.HBM
    operands = (
        token_ids,
        lengths,
        norm_gain,
        jnp.asarray(rotary_rates(HEAD_SIZE)),
        emb_table,
        q_weight,
        key_matrix,
        value_matrix,
        o_weight,
        key_cache.reshape(cache),
        value_cache.reshape(cache),
    )

    def run(compact):
        row_message = (2 * SLOTS, HEAD_SIZE) if compact else (ROWS, width)
        group_message = (2 * GROUP_SLOTS, HEAD_SIZE) if compact else (ROWS, width)
        return pl.pallas_call(
            functools.partial(kernel, compact),
            out_shape=(
                jax.ShapeDtypeStruct((ROWS // tp, width), BF16),
                jax.ShapeDtypeStruct((1,), jnp.int32),
            ),
            in_specs=[pl.BlockSpec(memory_space=m) for m in [smem, smem, vmem, vmem] + [hbm] * 7],
            out_specs=(pl.BlockSpec(memory_space=vmem), pl.BlockSpec(memory_space=smem)),
            scratch_shapes=[
                vmem((4, emb_table.shape[0], emb_table.shape[1] // 4), BF16),
                vmem((width, q_weight.shape[1] + 2 * HEAD_SIZE), BF16),
                vmem(o_weight.shape, BF16),
                vmem(cache, BF16),
                vmem((GAME_COUNT, key_cache.shape[1], 2 * HEAD_SIZE), BF16),
                vmem((seq,) + row_message, BF16),
                vmem((seq,) + row_message, BF16),
                vmem(group_message, BF16),
                vmem((tp,) + group_message, BF16),
                vmem((ROWS * 16, HEAD_SIZE), F32),
                vmem((ROWS, 16, HEAD_SIZE), BF16),
                vmem((seq, 16, HEAD_SIZE), BF16),
                vmem((ROWS, 8, HEAD_SIZE), BF16),
                vmem((2, 8, HEAD_SIZE), F32),
                vmem((GAME_COUNT, NEW_TOKENS * CANDIDATE_MOVES * GROUP, key_cache.shape[1]), F32),
                vmem((ROWS, 16, HEAD_SIZE), BF16),
                vmem((seq, 16, HEAD_SIZE), BF16),
                vmem((ROWS, 8, HEAD_SIZE), BF16),
                vmem((ROWS * 8, HEAD_SIZE), F32),
                vmem((tp, 8, HEAD_SIZE), F32),
                vmem((tp, 8, HEAD_SIZE), F32),
                pltpu.SemaphoreType.DMA((4,)),
                pltpu.SemaphoreType.DMA((6,)),
                pltpu.SemaphoreType.DMA((8,)),
                pltpu.SemaphoreType.DMA((8,)),
            ],
            compiler_params=pltpu.CompilerParams(
                collective_id=0 if compact else 1,
                has_side_effects=True,
                vmem_limit_bytes=64 * 1024 * 1024,
            ),
        )(*operands)

    result, overflow = run(True)
    return lax.cond(overflow[0] > 0, lambda: run(False)[0], lambda: result)


def solution(mesh):
    placed = (
        P(),
        P(),
        P("seq"),
        P(("seq", "tp"), None),
        P("seq", "tp"),
        P("seq", "tp"),
        P("seq", "tp"),
        P("tp", "seq"),
        P(None, "seq", "tp", None),
        P(None, "seq", "tp", None),
    )
    return jax.shard_map(
        local, mesh=mesh, in_specs=placed, out_specs=P("tp", "seq"), check_vma=False
    )
```

```python
import functools

import jax
import jax.numpy as jnp
import numpy as np
from jax import lax
from jax.experimental import pallas as pl
from jax.experimental.pallas import tpu as pltpu
from jax.sharding import PartitionSpec as P

MODEL_WIDTH = 8192
QUERY_HEADS = 64
KEY_HEADS = 8
HEAD_SIZE = 128
GAME_COUNT = 2
CANDIDATE_MOVES = 8
NEW_TOKENS = 2
ROWS = NEW_TOKENS * GAME_COUNT * CANDIDATE_MOVES
GROUP = QUERY_HEADS // KEY_HEADS

EPSILON = 1e-05
FLOOR = -1e30
LOWEST = -1e29
LOG2E = 1.4426950408889634
SLOTS = 4
GROUP_SLOTS = 12
KEYS = 1024
MESH = pl.DeviceIdType.MESH
F32 = jnp.float32
BF16 = jnp.bfloat16


def rotary_rates(head_dim):
    half_dim = head_dim // 2
    plain_rate = 500000.0 ** (-(np.arange(half_dim) * 2.0) / head_dim)
    wave_len = 2.0 * np.pi / plain_rate
    blend = (8192.0 / wave_len - 1.0) / 3.0
    scaled = np.where(
        wave_len < 2048.0,
        plain_rate,
        np.where(
            wave_len > 8192.0,
            plain_rate / 8.0,
            (1.0 - blend) * plain_rate / 8.0 + blend * plain_rate,
        ),
    )
    return np.concatenate([scaled, scaled]).astype(np.float32).reshape(1, head_dim)


def rounded(x):
    return x.astype(BF16).astype(F32)


def in_three(x):
    high = rounded(x)
    middle = rounded(x - high)
    return high, middle, rounded(x - high - middle)


def kernel(
    compact,
    ids,
    lengths,
    gain,
    rates,
    emb,
    q_weight,
    key_matrix,
    value_matrix,
    o_weight,
    key_cache,
    value_cache,
    out,
    overflow,
    table,
    weights,
    ow,
    kc,
    vc,
    send1,
    recv1,
    send2,
    recv2,
    spread,
    send3,
    recv3,
    rows,
    pair,
    scores,
    send5,
    recv5,
    send6,
    recv6,
    wide,
    send7,
    recv7,
    table_sems,
    load_sems,
    send_sems,
    recv_sems,
):
    seq, tp = lax.axis_size("seq"), lax.axis_size("tp")
    s, t = lax.axis_index("seq"), lax.axis_index("tp")
    width = gain.shape[0]
    vocab_local = emb.shape[0]
    heads = q_weight.shape[1]
    shard_len = key_cache.shape[1]
    scale = HEAD_SIZE ** (-0.5)

    y, x, core = lax.div(s, 8), lax.rem(lax.div(s, 2), 4), lax.rem(s, 2)

    def moved(dy, dx, dc):
        return (lax.rem(y + dy, 4) * 4 + lax.rem(x + dx, 4)) * 2 + lax.rem(core + dc, 2)

    steps = [(dy, dx, dc) for dy in range(4) for dx in range(4) for dc in range(2)]
    steps.sort(key=lambda d: -10 * (min(d[0], 4 - d[0]) + min(d[1], 4 - d[1])) - d[2])
    seq_peers = [moved(*d) for d in steps[:-1]]
    tp_peers = [lax.rem(t + d, tp) for d in (4, 3, 5, 2, 6, 1, 7)]

    planes = [lax.rem(y + dy, 4) for dy in (2, 1, 3, 0)]
    stripe = table.shape[2]
    table_loads = [
        pltpu.make_async_copy(
            emb.at[:, pl.ds(pl.multiple_of(plane * stripe, stripe), stripe)],
            table.at[i],
            table_sems.at[i],
        )
        for i, plane in enumerate(planes)
    ]
    for load in table_loads:
        load.start()

    barrier = pltpu.get_barrier_semaphore()

    greeted = [(s, peer) for peer in tp_peers]
    greeted = greeted[:3] + [(peer, t) for peer in seq_peers[:22]] + greeted[3:]
    for device in greeted + [(peer, t) for peer in seq_peers[22:]]:
        pl.semaphore_signal(barrier, inc=1, device_id=device, device_id_type=MESH)

    loads = [
        pltpu.make_async_copy(src, dst, load_sems.at[i])
        for i, (src, dst) in enumerate(
            [
                (q_weight, weights.at[:, pl.ds(0, heads)]),
                (key_matrix, weights.at[:, pl.ds(heads, HEAD_SIZE)]),
                (value_matrix, weights.at[:, pl.ds(heads + HEAD_SIZE, HEAD_SIZE)]),
                (key_cache, kc),
                (value_cache, vc.at[:, :, pl.ds(0, HEAD_SIZE)]),
                (o_weight, ow),
            ]
        )
    ]
    pending, loaded = [], set()

    def need(*names):
        for i in names:
            loads[i].wait()
            loaded.add(i)

    tokens = [ids[r // 16, (r // 8) % 2, r % 8] for r in range(ROWS)]
    down = jnp.zeros((ROWS, HEAD_SIZE), jnp.int32)
    along = jnp.zeros((ROWS, HEAD_SIZE), jnp.int32)
    rows_at = lax.broadcasted_iota(jnp.int32, (ROWS, HEAD_SIZE), 0)
    lanes_at = lax.broadcasted_iota(jnp.int32, (ROWS, HEAD_SIZE), 1)
    for r, token in enumerate(tokens):
        down = jnp.where(rows_at == r, token, down)
        along = jnp.where(lanes_at == r, token, along)
    in_block = vocab_local.bit_length() - 1
    block_down, block_along = jnp.right_shift(down, in_block), jnp.right_shift(along, in_block)
    plane_down, plane_along = block_down & (tp - 1), block_along & (tp - 1)
    first_id = (s * tp + t) * vocab_local
    token_rows = jnp.concatenate([down - first_id] * (vocab_local // HEAD_SIZE), axis=1)
    hits = jnp.where(
        token_rows == lax.broadcasted_iota(jnp.int32, (ROWS, vocab_local), 1), 1.0, 0.0
    ).astype(BF16)
    if compact:
        earlier, later = (lanes_at < rows_at), (rows_at < lanes_at)

        def slots(there, here):
            same = there == here
            by_row = jnp.sum(jnp.where(same & earlier, 1.0, 0.0), axis=1, keepdims=True)
            by_lane = jnp.sum(jnp.where(same & later, 1.0, 0.0), axis=0, keepdims=True)
            return by_row.astype(jnp.int32), by_lane.astype(jnp.int32)

        slot_down, slot_along = slots(block_down, block_along)
        group_down, group_along = slots(plane_down, plane_along)
        too_many = (jnp.max(slot_down) >= SLOTS) | (jnp.max(group_down) >= GROUP_SLOTS)
        overflow[0] = jnp.where(too_many, 1, 0)
        token_lane = lanes_at < ROWS
        mine = (block_along == s * tp + t) & (slot_along == rows_at) & token_lane
        mine = jnp.where(mine, 1.0, 0.0).astype(BF16)[:16, :ROWS]
        one_hot = jnp.dot(mine, hits, preferred_element_type=F32).astype(BF16)
        ours = (plane_along == t) & (group_along == rows_at) & token_lane
        ours = jnp.where(ours, 1.0, 0.0).astype(BF16)[:16, :ROWS]
        spot = jnp.right_shift(block_down[:, :1], tp.bit_length() - 1) * 2 * SLOTS + slot_down
        spots = lax.broadcasted_iota(jnp.int32, (ROWS, seq * 2 * SLOTS), 1)
        to_group = jnp.concatenate(
            [
                jnp.dot(
                    ours,
                    jnp.where(spots == spot + half * SLOTS, 1.0, 0.0).astype(BF16),
                    preferred_element_type=F32,
                )[:GROUP_SLOTS]
                for half in range(2)
            ],
            axis=0,
        ).astype(BF16)
        spot = plane_down[:, :1] * 2 * GROUP_SLOTS + group_down
        spots = lax.broadcasted_iota(jnp.int32, (ROWS, tp * 2 * GROUP_SLOTS), 1)
        to_rows = jnp.concatenate(
            [jnp.where(spots == spot + half * GROUP_SLOTS, 1.0, 0.0) for half in range(2)], axis=0
        ).astype(BF16)
    else:
        overflow[0] = 0
        one_hot = hits

    for i, plane in enumerate(planes):
        table_loads[i].wait()
        found = jnp.dot(one_hot, table[i], preferred_element_type=F32)
        for j in range(stripe // width):
            part = found[:, j * width : (j + 1) * width]
            if compact:
                part = jnp.concatenate(
                    [part[:SLOTS, :HEAD_SIZE], part[:SLOTS, HEAD_SIZE:]], axis=0
                )
            send1[plane * (stripe // width) + j] = part.astype(BF16)

    def scatter_copy(phase, source, target, device, arrival=None):
        return pltpu.make_async_remote_copy(
            src_ref=source,
            dst_ref=target,
            send_sem=send_sems.at[phase],
            recv_sem=recv_sems.at[phase if arrival is None else arrival],
            device_id=device,
            device_id_type=MESH,
        )

    def await_all(phase, buffer, count):
        part = buffer.at[pl.ds(0, count)]
        pltpu.make_async_copy(part, part, recv_sems.at[phase]).wait()

    def await_sent(phase, buffer, count):
        part = buffer.at[pl.ds(0, count)]
        pltpu.make_async_copy(part, part, send_sems.at[phase]).wait()

    pl.semaphore_wait(barrier, seq + tp - 2)

    for peer in seq_peers:
        scatter_copy(0, send1.at[peer], recv1.at[s], (peer, t)).start()
    pending.append(lambda: await_sent(0, send1, seq - 1))
    recv1[s] = send1[s]
    for load in loads:
        load.start()
    vc[:, :, HEAD_SIZE:] = jnp.ones((GAME_COUNT, shard_len, HEAD_SIZE), BF16)
    await_all(0, recv1, seq - 1)

    if compact:
        arrived = recv1[...].astype(F32).reshape(seq * 2 * SLOTS, HEAD_SIZE).astype(BF16)
        found = jnp.dot(to_group, arrived, preferred_element_type=F32).astype(BF16)
    else:
        found = jnp.sum(recv1[...].astype(F32), axis=0).astype(BF16)
    send2[...] = found
    for peer in tp_peers:
        scatter_copy(1, send2, recv2.at[t], (s, peer)).start()
    pending.append(lambda: await_sent(1, recv2, tp - 1))
    recv2[t] = found
    await_all(1, recv2, tp - 1)
    if compact:
        arrived = recv2[...].astype(F32).reshape(tp * 2 * GROUP_SLOTS, HEAD_SIZE).astype(BF16)
        embedded = jnp.dot(to_rows, arrived, preferred_element_type=F32)
        embedded = jnp.concatenate([embedded[:ROWS], embedded[ROWS:]], axis=1)
    else:
        embedded = jnp.sum(recv2[...].astype(F32), axis=0)

    squares = jnp.sum(embedded * embedded, axis=-1, keepdims=True)
    normed = (embedded * gain[...].astype(F32)[None, :]).astype(BF16)
    need(0, 1, 2)
    products = jnp.dot(normed, weights[...], preferred_element_type=F32)
    for j in range(GROUP + 2):
        spread[pl.ds(j, ROWS, stride=16), :] = products[:, j * HEAD_SIZE : (j + 1) * HEAD_SIZE]
    for j in range(10, 16):
        spread[pl.ds(j, ROWS, stride=16), :] = jnp.broadcast_to(squares, (ROWS, HEAD_SIZE))
    send3[...] = spread[...].reshape(ROWS, 16, HEAD_SIZE).astype(BF16)

    for peer in seq_peers:
        scatter_copy(2, send3.at[peer], recv3.at[s], (peer, t)).start()
    pending.append(lambda: await_sent(2, send3, seq - 1))
    recv3[s] = send3[s]
    game = lax.rem(lax.div(s, CANDIDATE_MOVES), GAME_COUNT)
    step = lax.div(s, GAME_COUNT * CANDIDATE_MOVES)
    position = (lengths[game] + step).astype(F32)
    angles = position * rates[...]
    lane = lax.broadcasted_iota(jnp.int32, (1, HEAD_SIZE), 1)
    cosine = jnp.cos(angles)
    sine = jnp.sin(angles)
    sine = jnp.where(lane < HEAD_SIZE // 2, -sine, sine)
    await_all(2, recv3, seq - 1)

    sums = jnp.sum(recv3[...].astype(F32), axis=0)
    inv_rms = lax.rsqrt(sums[10:11, :] / MODEL_WIDTH + EPSILON)
    scaled = sums * inv_rms
    turned = scaled * cosine + pltpu.roll(scaled, HEAD_SIZE // 2, 1) * sine
    place = lax.broadcasted_iota(jnp.int32, (16, HEAD_SIZE), 0)
    own = rounded(jnp.where(place < 9, turned, scaled))
    own_queries, own_pair = own[:8], own[8:]
    rows[s] = own_queries.astype(BF16)
    for peer in seq_peers:
        scatter_copy(3, rows.at[s], rows.at[s], (peer, t)).start()
    pending.append(lambda: await_sent(3, rows, seq - 1))
    pair[0] = own_pair
    twin = lax.rem(s + GAME_COUNT * CANDIDATE_MOVES, seq)
    twin_copy = scatter_copy(7, pair.at[0], pair.at[1], (twin, t))
    twin_copy.start()
    need(3, 4)
    await_all(3, rows, seq - 1)

    factor = scale * LOG2E
    games = range(GAME_COUNT)
    chunks = [pl.ds(i, KEYS) for i in range(0, shard_len, KEYS)]
    queries, peaks, tops, sums = [], [], [], []
    for g in games:
        halves = [
            rows[pl.ds(16 * a + 8 * g, 8)].astype(F32).reshape(64, HEAD_SIZE)
            for a in range(NEW_TOKENS)
        ]
        queries.append(jnp.concatenate(halves, axis=0).astype(BF16))
        peaks.append(jnp.full((128, HEAD_SIZE), FLOOR, F32))
    for chunk in chunks:
        slot = s * shard_len + chunk.start + lax.broadcasted_iota(jnp.int32, (1, KEYS), 1)
        for g in games:
            part = lax.dot_general(
                queries[g], kc[g, chunk, :], (((1,), (1,)), ((), ())), preferred_element_type=F32
            )
            part = jnp.where(slot < lengths[g], part, FLOOR)
            scores[g, :, chunk] = part
            for i in range(0, KEYS, HEAD_SIZE):
                peaks[g] = jnp.maximum(peaks[g], part[:, i : i + HEAD_SIZE])
    for g in games:
        tops.append(jnp.maximum(jnp.max(peaks[g], axis=-1, keepdims=True), LOWEST))
        sums.append(jnp.zeros((128, 2 * HEAD_SIZE), F32))
    for chunk in chunks:
        for g in games:
            shifted = jnp.exp2((scores[g, :, chunk] - tops[g]) * factor).astype(BF16)
            sums[g] += jnp.dot(shifted, vc[g, chunk, :], preferred_element_type=F32)
    lanes = lax.broadcasted_iota(jnp.int32, (128, HEAD_SIZE), 1)
    for g in games:
        top = jnp.broadcast_to(tops[g] * factor, (128, HEAD_SIZE))
        high, middle, low = in_three(jnp.where(lanes < 3, top, sums[g][:, HEAD_SIZE:]))
        turn = jnp.where(lanes < 3, lanes, lanes - 3)
        packed = jnp.where(turn == 0, high, jnp.where(turn == 1, middle, low))
        message = jnp.concatenate(
            [sums[g][:, :HEAD_SIZE].reshape(16, 8, HEAD_SIZE), packed.reshape(16, 8, HEAD_SIZE)],
            axis=1,
        ).astype(BF16)
        for a in range(NEW_TOKENS):
            send5[pl.ds(16 * a + 8 * g, 8)] = message[8 * a : 8 * a + 8]
    for peer in seq_peers:
        scatter_copy(4, send5.at[peer], recv5.at[s], (peer, t)).start()
    pending.append(lambda: await_sent(4, send5, seq - 1))
    recv5[s] = send5[s]

    twin_copy.wait()
    firsts = jnp.where(step >= 1, pair[1], own_pair)
    seconds = own_pair
    score_a = jnp.sum(own_queries * firsts[0:1, :], axis=-1, keepdims=True) * factor
    score_b = jnp.sum(own_queries * seconds[0:1, :], axis=-1, keepdims=True) * factor
    score_b = jnp.where(step >= 1, score_b, FLOOR)
    fresh_top = jnp.maximum(score_a, score_b)
    fresh_a = jnp.exp2(score_a - fresh_top)
    fresh_b = jnp.exp2(score_b - fresh_top)
    fresh_total = fresh_a + fresh_b
    fresh_sum = rounded(fresh_a) * firsts[1:2, :] + rounded(fresh_b) * seconds[1:2, :]
    pick = lax.broadcasted_iota(jnp.int32, (HEAD_SIZE, 2 * HEAD_SIZE), 0)
    side = lax.broadcasted_iota(jnp.int32, (HEAD_SIZE, 2 * HEAD_SIZE), 1) >= HEAD_SIZE
    pick = pick - jnp.where(side, 3, 0)
    picker = jnp.where((pick >= 0) & (pick < 3), 1.0, 0.0).astype(BF16)
    await_all(4, recv5, seq - 1)

    parts = recv5[...].astype(F32)
    unpacked = jnp.dot(
        parts[:, 8:, :].reshape(seq * 8, HEAD_SIZE).astype(BF16),
        picker,
        preferred_element_type=F32,
    )
    tops = unpacked[:, :HEAD_SIZE].reshape(seq, 8, HEAD_SIZE)
    totals = unpacked[:, HEAD_SIZE:].reshape(seq, 8, HEAD_SIZE)
    highest = jnp.maximum(jnp.max(tops, axis=0), fresh_top)
    shares = jnp.exp2(tops - highest[None])
    fresh_share = jnp.exp2(fresh_top - highest)
    whole = jnp.sum(shares * totals, axis=0) + fresh_share * fresh_total
    summed = jnp.sum(shares * parts[:, :8, :], axis=0) + fresh_share * fresh_sum
    share = ROWS // 8
    send6[...] = (summed / whole).astype(BF16)
    band = 8 + lax.div(s, share)
    pltpu.make_async_copy(send6, recv6.at[s], recv_sems.at[band]).start()
    for peer in seq_peers[22:] + seq_peers[:22]:
        scatter_copy(5, send6, recv6.at[s], (peer, t), band).start()
    pending.append(lambda: await_sent(5, recv6, seq - 1))
    need(5)

    for bands in ((0,), (1,), (2, 3), (4, 5, 6, 7)):
        for z in bands:
            await_all(8 + z, recv6, share)
        first, count = bands[0] * share, len(bands) * share
        wide[pl.ds(first * 8, count * 8), :] = (
            recv6[pl.ds(first, count)].astype(F32).reshape(count * 8, HEAD_SIZE)
        )
        contexts = jnp.concatenate(
            [wide[pl.ds(first * 8 + j, count, stride=8), :] for j in range(GROUP)], axis=1
        ).astype(BF16)
        product = jnp.dot(contexts, ow[...], preferred_element_type=F32)
        for i, z in enumerate(bands):
            send7[z, 0:share, :] = product[i * share : (i + 1) * share, :HEAD_SIZE]
            send7[z, share : 2 * share, :] = product[i * share : (i + 1) * share, HEAD_SIZE:]

            @pl.when(t != z)
            def _(z=z):
                scatter_copy(6, send7.at[z], recv7.at[t], (s, z)).start()

    pending.append(lambda: await_sent(6, send7, tp - 1))
    recv7[t] = send7[t]
    await_all(6, recv7, tp - 1)
    result = jnp.sum(recv7[...], axis=0)
    out[...] = jnp.concatenate([result[:share], result[share:]], axis=1).astype(BF16)

    for wait in pending:
        wait()


def local(
    token_ids,
    lengths,
    norm_gain,
    emb_table,
    q_weight,
    key_matrix,
    value_matrix,
    o_weight,
    key_cache,
    value_cache,
):
    seq, tp = lax.axis_size("seq"), lax.axis_size("tp")
    width = emb_table.shape[1] // seq
    cache = (GAME_COUNT, key_cache.shape[1], HEAD_SIZE)
    vmem, smem, hbm = pltpu.VMEM, pltpu.SMEM, pltpu.HBM
    operands = (
        token_ids,
        lengths,
        norm_gain,
        jnp.asarray(rotary_rates(HEAD_SIZE)),
        emb_table,
        q_weight,
        key_matrix,
        value_matrix,
        o_weight,
        key_cache.reshape(cache),
        value_cache.reshape(cache),
    )

    def run(compact):
        row_message = (2 * SLOTS, HEAD_SIZE) if compact else (ROWS, width)
        group_message = (2 * GROUP_SLOTS, HEAD_SIZE) if compact else (ROWS, width)
        return pl.pallas_call(
            functools.partial(kernel, compact),
            out_shape=(
                jax.ShapeDtypeStruct((ROWS // tp, width), BF16),
                jax.ShapeDtypeStruct((1,), jnp.int32),
            ),
            in_specs=[pl.BlockSpec(memory_space=m) for m in [smem, smem, vmem, vmem] + [hbm] * 7],
            out_specs=(pl.BlockSpec(memory_space=vmem), pl.BlockSpec(memory_space=smem)),
            scratch_shapes=[
                vmem((4, emb_table.shape[0], emb_table.shape[1] // 4), BF16),
                vmem((width, q_weight.shape[1] + 2 * HEAD_SIZE), BF16),
                vmem(o_weight.shape, BF16),
                vmem(cache, BF16),
                vmem((GAME_COUNT, key_cache.shape[1], 2 * HEAD_SIZE), BF16),
                vmem((seq,) + row_message, BF16),
                vmem((seq,) + row_message, BF16),
                vmem(group_message, BF16),
                vmem((tp,) + group_message, BF16),
                vmem((ROWS * 16, HEAD_SIZE), F32),
                vmem((ROWS, 16, HEAD_SIZE), BF16),
                vmem((seq, 16, HEAD_SIZE), BF16),
                vmem((ROWS, 8, HEAD_SIZE), BF16),
                vmem((2, 8, HEAD_SIZE), F32),
                vmem((GAME_COUNT, NEW_TOKENS * CANDIDATE_MOVES * GROUP, key_cache.shape[1]), F32),
                vmem((ROWS, 16, HEAD_SIZE), BF16),
                vmem((seq, 16, HEAD_SIZE), BF16),
                vmem((8, HEAD_SIZE), BF16),
                vmem((ROWS, 8, HEAD_SIZE), BF16),
                vmem((ROWS * 8, HEAD_SIZE), F32),
                vmem((tp, 8, HEAD_SIZE), F32),
                vmem((tp, 8, HEAD_SIZE), F32),
                pltpu.SemaphoreType.DMA((4,)),
                pltpu.SemaphoreType.DMA((6,)),
                pltpu.SemaphoreType.DMA((8,)),
                pltpu.SemaphoreType.DMA((16,)),
            ],
            compiler_params=pltpu.CompilerParams(
                collective_id=0 if compact else 1,
                has_side_effects=True,
                vmem_limit_bytes=64 * 1024 * 1024,
            ),
        )(*operands)

    result, overflow = run(True)
    return lax.cond(overflow[0] > 0, lambda: run(False)[0], lambda: result)


def solution(mesh):
    placed = (
        P(),
        P(),
        P("seq"),
        P(("seq", "tp"), None),
        P("seq", "tp"),
        P("seq", "tp"),
        P("seq", "tp"),
        P("tp", "seq"),
        P(None, "seq", "tp", None),
        P(None, "seq", "tp", None),
    )
    return jax.shard_map(
        local, mesh=mesh, in_specs=placed, out_specs=P("tp", "seq"), check_vma=False
    )
```

```python
import functools

import jax
import jax.numpy as jnp
import numpy as np
from jax import lax
from jax.experimental import pallas as pl
from jax.experimental.pallas import tpu as pltpu
from jax.sharding import PartitionSpec as P

MODEL_WIDTH = 8192
QUERY_HEADS = 64
KEY_HEADS = 8
HEAD_SIZE = 128
GAME_COUNT = 2
CANDIDATE_MOVES = 8
NEW_TOKENS = 2
ROWS = NEW_TOKENS * GAME_COUNT * CANDIDATE_MOVES
GROUP = QUERY_HEADS // KEY_HEADS

EPSILON = 1e-05
FLOOR = -1e30
LOWEST = -1e29
LOG2E = 1.4426950408889634
SLOTS = 4
GROUP_SLOTS = 12
KEYS = 1024
MESH = pl.DeviceIdType.MESH
F32 = jnp.float32
BF16 = jnp.bfloat16


def rotary_rates(head_dim):
    half_dim = head_dim // 2
    plain_rate = 500000.0 ** (-(np.arange(half_dim) * 2.0) / head_dim)
    wave_len = 2.0 * np.pi / plain_rate
    blend = (8192.0 / wave_len - 1.0) / 3.0
    scaled = np.where(
        wave_len < 2048.0,
        plain_rate,
        np.where(
            wave_len > 8192.0,
            plain_rate / 8.0,
            (1.0 - blend) * plain_rate / 8.0 + blend * plain_rate,
        ),
    )
    return np.concatenate([scaled, scaled]).astype(np.float32).reshape(1, head_dim)


def rounded(x):
    return x.astype(BF16).astype(F32)


def in_three(x):
    high = rounded(x)
    middle = rounded(x - high)
    return high, middle, rounded(x - high - middle)


def kernel(
    compact,
    ids,
    lengths,
    gain,
    rates,
    emb,
    q_weight,
    key_matrix,
    value_matrix,
    o_weight,
    key_cache,
    value_cache,
    out,
    overflow,
    table,
    weights,
    ow,
    kc,
    vc,
    send1,
    recv1,
    send2,
    recv2,
    spread,
    send3,
    recv3,
    rows,
    pair,
    scores,
    send5,
    recv5,
    send6,
    recv6,
    wide,
    send7,
    recv7,
    table_sems,
    load_sems,
    send_sems,
    recv_sems,
):
    seq, tp = lax.axis_size("seq"), lax.axis_size("tp")
    s, t = lax.axis_index("seq"), lax.axis_index("tp")
    width = gain.shape[0]
    vocab_local = emb.shape[0]
    heads = q_weight.shape[1]
    shard_len = key_cache.shape[1]
    scale = HEAD_SIZE ** (-0.5)

    y, x, core = lax.div(s, 8), lax.rem(lax.div(s, 2), 4), lax.rem(s, 2)

    def moved(dy, dx, dc):
        return (lax.rem(y + dy, 4) * 4 + lax.rem(x + dx, 4)) * 2 + lax.rem(core + dc, 2)

    steps = [(dy, dx, dc) for dy in range(4) for dx in range(4) for dc in range(2)]
    steps.sort(key=lambda d: -10 * (min(d[0], 4 - d[0]) + min(d[1], 4 - d[1])) - d[2])
    seq_peers = [moved(*d) for d in steps[:-1]]
    tp_peers = [lax.rem(t + d, tp) for d in (4, 3, 5, 2, 6, 1, 7)]

    planes = [lax.rem(y + dy, 4) for dy in (2, 1, 3, 0)]
    stripe = table.shape[2]
    table_loads = [
        pltpu.make_async_copy(
            emb.at[:, pl.ds(pl.multiple_of(plane * stripe, stripe), stripe)],
            table.at[i],
            table_sems.at[i],
        )
        for i, plane in enumerate(planes)
    ]
    for load in table_loads:
        load.start()

    barrier = pltpu.get_barrier_semaphore()

    greeted = [(s, peer) for peer in tp_peers]
    greeted = greeted[:3] + [(peer, t) for peer in seq_peers[:22]] + greeted[3:]
    for device in greeted + [(peer, t) for peer in seq_peers[22:]]:
        pl.semaphore_signal(barrier, inc=1, device_id=device, device_id_type=MESH)

    loads = [
        pltpu.make_async_copy(src, dst, load_sems.at[i])
        for i, (src, dst) in enumerate(
            [
                (q_weight, weights.at[:, pl.ds(0, heads)]),
                (key_matrix, weights.at[:, pl.ds(heads, HEAD_SIZE)]),
                (value_matrix, weights.at[:, pl.ds(heads + HEAD_SIZE, HEAD_SIZE)]),
                (key_cache, kc),
                (value_cache, vc.at[:, :, pl.ds(0, HEAD_SIZE)]),
                (o_weight, ow),
            ]
        )
    ]
    pending, loaded = [], set()

    def need(*names):
        for i in names:
            loads[i].wait()
            loaded.add(i)

    tokens = [ids[r // 16, (r // 8) % 2, r % 8] for r in range(ROWS)]
    down = jnp.zeros((ROWS, HEAD_SIZE), jnp.int32)
    along = jnp.zeros((ROWS, HEAD_SIZE), jnp.int32)
    rows_at = lax.broadcasted_iota(jnp.int32, (ROWS, HEAD_SIZE), 0)
    lanes_at = lax.broadcasted_iota(jnp.int32, (ROWS, HEAD_SIZE), 1)
    for r, token in enumerate(tokens):
        down = jnp.where(rows_at == r, token, down)
        along = jnp.where(lanes_at == r, token, along)
    in_block = vocab_local.bit_length() - 1
    block_down, block_along = jnp.right_shift(down, in_block), jnp.right_shift(along, in_block)
    plane_down, plane_along = block_down & (tp - 1), block_along & (tp - 1)
    first_id = (s * tp + t) * vocab_local
    token_rows = jnp.concatenate([down - first_id] * (vocab_local // HEAD_SIZE), axis=1)
    hits = jnp.where(
        token_rows == lax.broadcasted_iota(jnp.int32, (ROWS, vocab_local), 1), 1.0, 0.0
    ).astype(BF16)
    if compact:
        earlier, later = (lanes_at < rows_at), (rows_at < lanes_at)

        def slots(there, here):
            same = there == here
            by_row = jnp.sum(jnp.where(same & earlier, 1.0, 0.0), axis=1, keepdims=True)
            by_lane = jnp.sum(jnp.where(same & later, 1.0, 0.0), axis=0, keepdims=True)
            return by_row.astype(jnp.int32), by_lane.astype(jnp.int32)

        slot_down, slot_along = slots(block_down, block_along)
        group_down, group_along = slots(plane_down, plane_along)
        too_many = (jnp.max(slot_down) >= SLOTS) | (jnp.max(group_down) >= GROUP_SLOTS)
        overflow[0] = jnp.where(too_many, 1, 0)
        token_lane = lanes_at < ROWS
        mine = (block_along == s * tp + t) & (slot_along == rows_at) & token_lane
        mine = jnp.where(mine, 1.0, 0.0).astype(BF16)[:16, :ROWS]
        one_hot = jnp.dot(mine, hits, preferred_element_type=F32).astype(BF16)
        ours = (plane_along == t) & (group_along == rows_at) & token_lane
        ours = jnp.where(ours, 1.0, 0.0).astype(BF16)[:16, :ROWS]
        spot = jnp.right_shift(block_down[:, :1], tp.bit_length() - 1) * 2 * SLOTS + slot_down
        spots = lax.broadcasted_iota(jnp.int32, (ROWS, seq * 2 * SLOTS), 1)
        to_group = jnp.concatenate(
            [
                jnp.dot(
                    ours,
                    jnp.where(spots == spot + half * SLOTS, 1.0, 0.0).astype(BF16),
                    preferred_element_type=F32,
                )[:GROUP_SLOTS]
                for half in range(2)
            ],
            axis=0,
        ).astype(BF16)
        spot = plane_down[:, :1] * 2 * GROUP_SLOTS + group_down
        spots = lax.broadcasted_iota(jnp.int32, (ROWS, tp * 2 * GROUP_SLOTS), 1)
        to_rows = jnp.concatenate(
            [jnp.where(spots == spot + half * GROUP_SLOTS, 1.0, 0.0) for half in range(2)], axis=0
        ).astype(BF16)
    else:
        overflow[0] = 0
        one_hot = hits

    for i, plane in enumerate(planes):
        table_loads[i].wait()
        found = jnp.dot(one_hot, table[i], preferred_element_type=F32)
        for j in range(stripe // width):
            part = found[:, j * width : (j + 1) * width]
            if compact:
                part = jnp.concatenate(
                    [part[:SLOTS, :HEAD_SIZE], part[:SLOTS, HEAD_SIZE:]], axis=0
                )
            send1[plane * (stripe // width) + j] = part.astype(BF16)

    def scatter_copy(phase, source, target, device, arrival=None):
        return pltpu.make_async_remote_copy(
            src_ref=source,
            dst_ref=target,
            send_sem=send_sems.at[phase],
            recv_sem=recv_sems.at[phase if arrival is None else arrival],
            device_id=device,
            device_id_type=MESH,
        )

    def await_all(phase, buffer, count):
        part = buffer.at[pl.ds(0, count)]
        pltpu.make_async_copy(part, part, recv_sems.at[phase]).wait()

    def await_sent(phase, buffer, count):
        part = buffer.at[pl.ds(0, count)]
        pltpu.make_async_copy(part, part, send_sems.at[phase]).wait()

    pl.semaphore_wait(barrier, seq + tp - 2)

    for peer in seq_peers:
        scatter_copy(0, send1.at[peer], recv1.at[s], (peer, t)).start()
    pending.append(lambda: await_sent(0, send1, seq - 1))
    recv1[s] = send1[s]
    for load in loads:
        load.start()
    vc[:, :, HEAD_SIZE:] = jnp.ones((GAME_COUNT, shard_len, HEAD_SIZE), BF16)
    await_all(0, recv1, seq - 1)

    if compact:
        arrived = recv1[...].astype(F32).reshape(seq * 2 * SLOTS, HEAD_SIZE).astype(BF16)
        found = jnp.dot(to_group, arrived, preferred_element_type=F32).astype(BF16)
    else:
        found = jnp.sum(recv1[...].astype(F32), axis=0).astype(BF16)
    send2[...] = found
    for peer in tp_peers:
        scatter_copy(1, send2, recv2.at[t], (s, peer)).start()
    pending.append(lambda: await_sent(1, recv2, tp - 1))
    recv2[t] = found
    await_all(1, recv2, tp - 1)
    if compact:
        arrived = recv2[...].astype(F32).reshape(tp * 2 * GROUP_SLOTS, HEAD_SIZE).astype(BF16)
        embedded = jnp.dot(to_rows, arrived, preferred_element_type=F32)
        embedded = jnp.concatenate([embedded[:ROWS], embedded[ROWS:]], axis=1)
    else:
        embedded = jnp.sum(recv2[...].astype(F32), axis=0)

    squares = jnp.sum(embedded * embedded, axis=-1, keepdims=True)
    normed = (embedded * gain[...].astype(F32)[None, :]).astype(BF16)
    need(0, 1, 2)
    products = jnp.dot(normed, weights[...], preferred_element_type=F32)
    for j in range(GROUP + 2):
        spread[pl.ds(j, ROWS, stride=16), :] = products[:, j * HEAD_SIZE : (j + 1) * HEAD_SIZE]
    for j in range(10, 16):
        spread[pl.ds(j, ROWS, stride=16), :] = jnp.broadcast_to(squares, (ROWS, HEAD_SIZE))
    send3[...] = spread[...].reshape(ROWS, 16, HEAD_SIZE).astype(BF16)

    for peer in seq_peers:
        scatter_copy(2, send3.at[peer], recv3.at[s], (peer, t)).start()
    pending.append(lambda: await_sent(2, send3, seq - 1))
    recv3[s] = send3[s]
    game = lax.rem(lax.div(s, CANDIDATE_MOVES), GAME_COUNT)
    step = lax.div(s, GAME_COUNT * CANDIDATE_MOVES)
    position = (lengths[game] + step).astype(F32)
    angles = position * rates[...]
    lane = lax.broadcasted_iota(jnp.int32, (1, HEAD_SIZE), 1)
    cosine = jnp.cos(angles)
    sine = jnp.sin(angles)
    sine = jnp.where(lane < HEAD_SIZE // 2, -sine, sine)
    await_all(2, recv3, seq - 1)

    sums = jnp.sum(recv3[...].astype(F32), axis=0)
    inv_rms = lax.rsqrt(sums[10:11, :] / MODEL_WIDTH + EPSILON)
    scaled = sums * inv_rms
    turned = scaled * cosine + pltpu.roll(scaled, HEAD_SIZE // 2, 1) * sine
    place = lax.broadcasted_iota(jnp.int32, (16, HEAD_SIZE), 0)
    own = rounded(jnp.where(place < 9, turned, scaled))
    own_queries, own_pair = own[:8], own[8:]
    rows[s] = own_queries.astype(BF16)
    for peer in seq_peers:
        scatter_copy(3, rows.at[s], rows.at[s], (peer, t)).start()
    pending.append(lambda: await_sent(3, rows, seq - 1))
    pair[0] = own_pair
    twin = lax.rem(s + GAME_COUNT * CANDIDATE_MOVES, seq)
    twin_copy = scatter_copy(7, pair.at[0], pair.at[1], (twin, t))
    twin_copy.start()
    need(3, 4)
    await_all(3, rows, seq - 1)

    factor = scale * LOG2E
    games = range(GAME_COUNT)
    chunks = [pl.ds(i, KEYS) for i in range(0, shard_len, KEYS)]
    queries, peaks, tops, sums = [], [], [], []
    for g in games:
        halves = [
            rows[pl.ds(16 * a + 8 * g, 8)].astype(F32).reshape(64, HEAD_SIZE)
            for a in range(NEW_TOKENS)
        ]
        queries.append(jnp.concatenate(halves, axis=0).astype(BF16))
        peaks.append(jnp.full((128, HEAD_SIZE), FLOOR, F32))
    def score(g, chunk):
        slot = s * shard_len + chunk.start + lax.broadcasted_iota(jnp.int32, (1, KEYS), 1)
        part = lax.dot_general(
            queries[g], kc[g, chunk, :], (((1,), (1,)), ((), ())), preferred_element_type=F32
        )
        part = jnp.where(slot < lengths[g], part, FLOOR)
        scores[g, :, chunk] = part
        for i in range(0, KEYS, HEAD_SIZE):
            peaks[g] = jnp.maximum(peaks[g], part[:, i : i + HEAD_SIZE])

    def settle(g):
        tops.append(jnp.maximum(jnp.max(peaks[g], axis=-1, keepdims=True), LOWEST))
        sums.append(jnp.zeros((128, 2 * HEAD_SIZE), F32))

    def gather(g, chunk):
        shifted = jnp.exp2((scores[g, :, chunk] - tops[g]) * factor).astype(BF16)
        sums[g] += jnp.dot(shifted, vc[g, chunk, :], preferred_element_type=F32)

    def send_parts(g):
        lanes = lax.broadcasted_iota(jnp.int32, (128, HEAD_SIZE), 1)
        top = jnp.broadcast_to(tops[g] * factor, (128, HEAD_SIZE))
        high, middle, low = in_three(jnp.where(lanes < 3, top, sums[g][:, HEAD_SIZE:]))
        turn = jnp.where(lanes < 3, lanes, lanes - 3)
        packed = jnp.where(turn == 0, high, jnp.where(turn == 1, middle, low))
        message = jnp.concatenate(
            [sums[g][:, :HEAD_SIZE].reshape(16, 8, HEAD_SIZE), packed.reshape(16, 8, HEAD_SIZE)],
            axis=1,
        ).astype(BF16)
        for a in range(NEW_TOKENS):
            send5[pl.ds(16 * a + 8 * g, 8)] = message[8 * a : 8 * a + 8]
        half = lax.div(y, 2)
        places = [(i, dx, dc) for i in range(2) for dx in (2, 1, 3, 0) for dc in (1, 0)]
        for i, dx, dc in places:
            plane = g + 2 * (half if i else 1 - half)
            peer = (plane * 4 + lax.rem(x + dx, 4)) * 2 + lax.rem(core + dc, 2)

            def start(peer=peer):
                scatter_copy(4, send5.at[peer], recv5.at[s], (peer, t)).start()

            if (i, dx, dc) == places[-1]:
                pl.when(peer != s)(start)
            else:
                start()

    for chunk in chunks:
        score(0, chunk)
    settle(0)
    for chunk in chunks:
        gather(0, chunk)
        score(1, chunk)
    send_parts(0)
    settle(1)
    for chunk in chunks:
        gather(1, chunk)
    send_parts(1)
    pending.append(lambda: await_sent(4, send5, seq - 1))
    recv5[s] = send5[s]

    twin_copy.wait()
    firsts = jnp.where(step >= 1, pair[1], own_pair)
    seconds = own_pair
    score_a = jnp.sum(own_queries * firsts[0:1, :], axis=-1, keepdims=True) * factor
    score_b = jnp.sum(own_queries * seconds[0:1, :], axis=-1, keepdims=True) * factor
    score_b = jnp.where(step >= 1, score_b, FLOOR)
    fresh_top = jnp.maximum(score_a, score_b)
    fresh_a = jnp.exp2(score_a - fresh_top)
    fresh_b = jnp.exp2(score_b - fresh_top)
    fresh_total = fresh_a + fresh_b
    fresh_sum = rounded(fresh_a) * firsts[1:2, :] + rounded(fresh_b) * seconds[1:2, :]
    pick = lax.broadcasted_iota(jnp.int32, (HEAD_SIZE, 2 * HEAD_SIZE), 0)
    side = lax.broadcasted_iota(jnp.int32, (HEAD_SIZE, 2 * HEAD_SIZE), 1) >= HEAD_SIZE
    pick = pick - jnp.where(side, 3, 0)
    picker = jnp.where((pick >= 0) & (pick < 3), 1.0, 0.0).astype(BF16)
    await_all(4, recv5, seq - 1)

    parts = recv5[...].astype(F32)
    unpacked = jnp.dot(
        parts[:, 8:, :].reshape(seq * 8, HEAD_SIZE).astype(BF16),
        picker,
        preferred_element_type=F32,
    )
    tops = unpacked[:, :HEAD_SIZE].reshape(seq, 8, HEAD_SIZE)
    totals = unpacked[:, HEAD_SIZE:].reshape(seq, 8, HEAD_SIZE)
    highest = jnp.maximum(jnp.max(tops, axis=0), fresh_top)
    shares = jnp.exp2(tops - highest[None])
    fresh_share = jnp.exp2(fresh_top - highest)
    whole = jnp.sum(shares * totals, axis=0) + fresh_share * fresh_total
    summed = jnp.sum(shares * parts[:, :8, :], axis=0) + fresh_share * fresh_sum
    share = ROWS // 8
    send6[...] = (summed / whole).astype(BF16)
    band = 8 + lax.div(s, share)
    pltpu.make_async_copy(send6, recv6.at[s], recv_sems.at[band]).start()
    first_to_send = seq_peers[22:] + [moved(0, 2, 1), moved(0, 2, 0)]
    for peer in first_to_send + [p for i, p in enumerate(seq_peers[:22]) if i not in (10, 16)]:
        scatter_copy(5, send6, recv6.at[s], (peer, t), band).start()
    pending.append(lambda: await_sent(5, recv6, seq - 1))
    need(5)

    for bands in ((0,), (1,), (2,), (3,), (4, 5, 6, 7)):
        for z in bands:
            await_all(8 + z, recv6, share)
        first, count = bands[0] * share, len(bands) * share
        wide[pl.ds(first * 8, count * 8), :] = (
            recv6[pl.ds(first, count)].astype(F32).reshape(count * 8, HEAD_SIZE)
        )
        contexts = jnp.concatenate(
            [wide[pl.ds(first * 8 + j, count, stride=8), :] for j in range(GROUP)], axis=1
        ).astype(BF16)
        product = jnp.dot(contexts, ow[...], preferred_element_type=F32)
        for i, z in enumerate(bands):
            send7[z, 0:share, :] = product[i * share : (i + 1) * share, :HEAD_SIZE]
            send7[z, share : 2 * share, :] = product[i * share : (i + 1) * share, HEAD_SIZE:]

            @pl.when(t != z)
            def _(z=z):
                scatter_copy(6, send7.at[z], recv7.at[t], (s, z)).start()

    pending.append(lambda: await_sent(6, send7, tp - 1))
    recv7[t] = send7[t]
    await_all(6, recv7, tp - 1)
    result = jnp.sum(recv7[...], axis=0)
    out[...] = jnp.concatenate([result[:share], result[share:]], axis=1).astype(BF16)

    for wait in pending:
        wait()


def local(
    token_ids,
    lengths,
    norm_gain,
    emb_table,
    q_weight,
    key_matrix,
    value_matrix,
    o_weight,
    key_cache,
    value_cache,
):
    seq, tp = lax.axis_size("seq"), lax.axis_size("tp")
    width = emb_table.shape[1] // seq
    cache = (GAME_COUNT, key_cache.shape[1], HEAD_SIZE)
    vmem, smem, hbm = pltpu.VMEM, pltpu.SMEM, pltpu.HBM
    operands = (
        token_ids,
        lengths,
        norm_gain,
        jnp.asarray(rotary_rates(HEAD_SIZE)),
        emb_table,
        q_weight,
        key_matrix,
        value_matrix,
        o_weight,
        key_cache.reshape(cache),
        value_cache.reshape(cache),
    )

    def run(compact):
        row_message = (2 * SLOTS, HEAD_SIZE) if compact else (ROWS, width)
        group_message = (2 * GROUP_SLOTS, HEAD_SIZE) if compact else (ROWS, width)
        return pl.pallas_call(
            functools.partial(kernel, compact),
            out_shape=(
                jax.ShapeDtypeStruct((ROWS // tp, width), BF16),
                jax.ShapeDtypeStruct((1,), jnp.int32),
            ),
            in_specs=[pl.BlockSpec(memory_space=m) for m in [smem, smem, vmem, vmem] + [hbm] * 7],
            out_specs=(pl.BlockSpec(memory_space=vmem), pl.BlockSpec(memory_space=smem)),
            scratch_shapes=[
                vmem((4, emb_table.shape[0], emb_table.shape[1] // 4), BF16),
                vmem((width, q_weight.shape[1] + 2 * HEAD_SIZE), BF16),
                vmem(o_weight.shape, BF16),
                vmem(cache, BF16),
                vmem((GAME_COUNT, key_cache.shape[1], 2 * HEAD_SIZE), BF16),
                vmem((seq,) + row_message, BF16),
                vmem((seq,) + row_message, BF16),
                vmem(group_message, BF16),
                vmem((tp,) + group_message, BF16),
                vmem((ROWS * 16, HEAD_SIZE), F32),
                vmem((ROWS, 16, HEAD_SIZE), BF16),
                vmem((seq, 16, HEAD_SIZE), BF16),
                vmem((ROWS, 8, HEAD_SIZE), BF16),
                vmem((2, 8, HEAD_SIZE), F32),
                vmem((GAME_COUNT, NEW_TOKENS * CANDIDATE_MOVES * GROUP, key_cache.shape[1]), F32),
                vmem((ROWS, 16, HEAD_SIZE), BF16),
                vmem((seq, 16, HEAD_SIZE), BF16),
                vmem((8, HEAD_SIZE), BF16),
                vmem((ROWS, 8, HEAD_SIZE), BF16),
                vmem((ROWS * 8, HEAD_SIZE), F32),
                vmem((tp, 8, HEAD_SIZE), F32),
                vmem((tp, 8, HEAD_SIZE), F32),
                pltpu.SemaphoreType.DMA((4,)),
                pltpu.SemaphoreType.DMA((6,)),
                pltpu.SemaphoreType.DMA((8,)),
                pltpu.SemaphoreType.DMA((16,)),
            ],
            compiler_params=pltpu.CompilerParams(
                collective_id=0 if compact else 1,
                has_side_effects=True,
                vmem_limit_bytes=64 * 1024 * 1024,
            ),
        )(*operands)

    result, overflow = run(True)
    return lax.cond(overflow[0] > 0, lambda: run(False)[0], lambda: result)


def solution(mesh):
    placed = (
        P(),
        P(),
        P("seq"),
        P(("seq", "tp"), None),
        P("seq", "tp"),
        P("seq", "tp"),
        P("seq", "tp"),
        P("tp", "seq"),
        P(None, "seq", "tp", None),
        P(None, "seq", "tp", None),
    )
    return jax.shard_map(
        local, mesh=mesh, in_specs=placed, out_specs=P("tp", "seq"), check_vma=False
    )
```
